256 devices in a mesh: tile: 128 (over x, y, z_hi, core), slab: 2 (over z_lo).
Axes of the slice: x: 4, y: 4, z: 8 (z_hi: 4, z_lo: 2; z = z_hi * 2 + z_lo), core: 2. Of those that a mesh axis runs over, the one named last changes fastest.
Arguments:
- volume: bfloat16 [128, 128, 2048], P('tile', 'slab'), may hold values from -6 to 6
- fov_mask: int32 [128, 2048], P('tile'), may hold values from 0 to 1, as said below
- block_angles: int32 [16], replicated, may hold values from 0 to 149
- row_range: int32 [128, 2], replicated, may hold values from 0 to 64, as said below
Outputs:
- sinogram: float32 [128, 64, 1024], P('tile', 'slab')
The draws below stay inside these ranges and needn't reach their ends.
Inputs may be any that keep to these rules, and one draw needn't show every extreme that they name: fov_mask[t, p] is 1 exactly where the voxel lies inside a region about the volume's centre whose extent along y is set separately for each voxel column x. row_range[v, 0] < row_range[v, 1] for every view.
All inputs are finite; a program needn't handle non-finite values.
Results may differ from the reference program's by a relative error of at most 0.0029.
Values sent between devices are 32-bit elements; how exact they have to be, the bound alone decides.
A program may use at most 64 MiB of HBM per device.

```python
import math
import jax
import jax.numpy as jnp
from jax import lax

COLS = 1024
WIN = 128
R_SLAB = 32
TX = 32
TY = 64
GRID_X = 16
CZ = 64
TILES = 128
VIEWS = 128
BLOCKS = 16
ROWS = 64
NZ = 128
NXV = 512
NYV = 512
PIX = 2048


def draw_fov_mask(key, part):
    key = jax.random.fold_in(key, 11)
    low_bound = (2 * (NXV * 5 // 16)) ** 2
    high_bound = (2 * (NXV * 7 // 16)) ** 2 + 1
    column_reach = jax.random.randint(key, (NXV,), low_bound, high_bound)
    tile_ids = jnp.arange(TILES, dtype=jnp.int32)[:, None]
    pixels = jnp.arange(PIX, dtype=jnp.int32)[None, :]
    grid_row = tile_ids // GRID_X
    along_row = tile_ids % GRID_X
    grid_col = jnp.where(grid_row % 2 == 0, along_row, GRID_X - 1 - along_row)
    x_index = grid_col * TX + pixels // TY
    x_off = 2 * x_index + 1 - NXV
    y_off = 2 * (grid_row * TY + pixels % TY) + 1 - NYV
    reach = column_reach[x_index]
    return (x_off * x_off + y_off * y_off <= reach).astype(jnp.int32)


def draw_row_range(key, part):
    key = jax.random.fold_in(key, 23)
    key_low, key_high, key_first, key_last = jax.random.split(key, 4)
    low_rows = jax.random.randint(key_low, (VIEWS,), 0, ROWS // 4)
    high_rows = ROWS - jax.random.randint(key_high, (VIEWS,), 0, ROWS // 4)
    view_ids = jnp.arange(VIEWS, dtype=jnp.int32)
    pick_low = jax.random.randint(key_first, (), 0, VIEWS)
    pick_high = jax.random.randint(key_last, (), 0, VIEWS)
    low_rows = jnp.where(view_ids == pick_low, 0, low_rows)
    high_rows = jnp.where(view_ids == pick_high, ROWS, high_rows)
    return jnp.stack([low_rows, high_rows], axis=1).astype(jnp.int32)


def with_ends(entries, rng, least, top_value):
    shape = entries.shape
    spot = [jax.random.randint(jax.random.fold_in(rng, axis), (), 0, shape[axis]) for axis in range(len(shape))]
    entries = entries.at[tuple(spot)].set(least)
    longest = shape.index(max(shape))
    spot[longest] = (spot[longest] + 1) % shape[longest]
    return entries.at[tuple(spot)].set(top_value)


def block_scale(key, extent, pieces, low, high):
    loudness = 1.0
    for position, blocks in pieces:
        heights = jax.random.uniform(jax.random.fold_in(jax.random.fold_in(key, 6), position), (blocks,), jnp.float32, low / len(pieces), high / len(pieces))
        loudness = loudness * jnp.repeat(jnp.exp(heights), extent[position] // blocks).reshape((-1,) + (1,) * (len(extent) - 1 - position))
    return loudness


def gaussian(key, dims, scale, bound, cuts=(), held_as=jnp.bfloat16):
    array = scale * jax.random.normal(key, dims, jnp.float32)
    if cuts:
        array = array * block_scale(key, dims, cuts, -0.22, 0.18)
    return jnp.clip(array, -bound, bound).astype(held_as)


def setup_inputs(seed: int = 0) -> dict:
    key_list = jax.random.split(jax.random.key(seed), 5)
    return {
        "volume": gaussian(key_list[0], (TILES, NZ, PIX), 1.0, 6.0, ((0, 128), (1, 2))),
        "fov_mask": draw_fov_mask(jax.random.fold_in(key_list[4], 71), 0),
        "block_angles": with_ends(jax.random.randint(key_list[2], (BLOCKS,), 0, 150), jax.random.fold_in(key_list[2], 1), 0, 149).astype(jnp.int32),
        "row_range": draw_row_range(jax.random.fold_in(key_list[4], 71), 0),
    }


def view_geometry(block_angles, view_id):
    angle_index = block_angles[view_id // 8] + 150 * (view_id % 8)
    angle_rad = angle_index.astype(jnp.float32) * (2.0 * math.pi / 1200.0)
    cos_part = jnp.cos(angle_rad)
    sin_part = jnp.sin(angle_rad)
    spread = jnp.maximum(jnp.abs(cos_part), jnp.abs(sin_part))
    magnify = 1.3 + 0.35 * cos_part
    return (cos_part, sin_part, magnify, magnify * spread, 1.0 / spread, 2.5 * sin_part, (R_SLAB / CZ) * magnify / 1.65)


def snake_position(tile_id):
    grid_row = tile_id // GRID_X
    along_row = tile_id % GRID_X
    grid_col = jnp.where(grid_row % 2 == 0, along_row, GRID_X - 1 - along_row)
    return grid_col, grid_row


def transaxial(grid_col, grid_row, geometry, half_x, half_y):
    cos_part, sin_part, magnify, box_width, amplitude = geometry[:5]
    pixels = jnp.arange(TX * TY, dtype=jnp.int32)
    x_pos = (grid_col * TX + pixels // TY).astype(jnp.float32) + 0.5 - half_x
    y_pos = (grid_row * TY + pixels % TY).astype(jnp.float32) + 0.5 - half_y
    centre = COLS / 2 + magnify * (x_pos * cos_part + y_pos * sin_part)
    tile_x = (grid_col * TX).astype(jnp.float32) + TX / 2 - half_x
    tile_y = (grid_row * TY).astype(jnp.float32) + TY / 2 - half_y
    tile_centre = COLS / 2 + magnify * (tile_x * cos_part + tile_y * sin_part)
    first_col = jnp.clip(jnp.floor(tile_centre).astype(jnp.int32) - WIN // 2, 0, COLS - WIN)
    col_edges = (first_col + jnp.arange(WIN, dtype=jnp.int32)).astype(jnp.float32)
    low_end = jnp.maximum(centre[:, None] - box_width / 2, col_edges[None, :])
    high_end = jnp.minimum(centre[:, None] + box_width / 2, col_edges[None, :] + 1.0)
    footprint = (jnp.maximum(high_end - low_end, 0.0) * amplitude).astype(jnp.bfloat16)
    return footprint, first_col


def axial_footprint(row_index, z_pos, geometry, total_rows):
    row_shift, axial_width = geometry[5], geometry[6]
    centre = total_rows / 2 + row_shift + axial_width * z_pos
    row_float = row_index.astype(jnp.float32)
    low_end = jnp.maximum(centre[None, :] - axial_width / 2, row_float[:, None])
    high_end = jnp.minimum(centre[None, :] + axial_width / 2, row_float[:, None] + 1.0)
    return jnp.maximum(high_end - low_end, 0.0)


def reference(volume, fov_mask, block_angles, row_range):
    masked = (volume * fov_mask[:, None, :].astype(jnp.bfloat16)).astype(jnp.float32)
    tile_ids = jnp.arange(TILES, dtype=jnp.int32)
    grid_col, grid_row = snake_position(tile_ids)
    row_index = jnp.arange(ROWS, dtype=jnp.int32)
    z_pos = jnp.arange(NZ, dtype=jnp.int32).astype(jnp.float32) + 0.5 - NZ / 2

    def one_view(view_id):
        geometry = view_geometry(block_angles, view_id)
        footprint, first_col = jax.vmap(transaxial, in_axes=(0, 0, None, None, None))(grid_col, grid_row, geometry, NXV / 2, NYV / 2)
        partial_value = jnp.einsum("tzp,tpw->tzw", masked, footprint.astype(jnp.float32), precision=lax.Precision.HIGHEST)
        weights = axial_footprint(row_index, z_pos, geometry, ROWS)
        band_sum = jnp.einsum("rz,tzw->trw", weights, partial_value, precision=lax.Precision.HIGHEST)

        def place_tile(tile_id, sinogram):
            start_col = first_col[tile_id]
            current = lax.dynamic_slice(sinogram, (jnp.int32(0), start_col), (ROWS, WIN))
            return lax.dynamic_update_slice(sinogram, current + band_sum[tile_id], (jnp.int32(0), start_col))

        sinogram = lax.fori_loop(0, TILES, place_tile, jnp.zeros((ROWS, COLS), jnp.float32))
        in_range = (row_index >= row_range[view_id, 0]) & (row_index < row_range[view_id, 1])
        return jnp.where(in_range[:, None], sinogram, jnp.float32(0.0))

    return lax.map(one_view, jnp.arange(VIEWS, dtype=jnp.int32))
```

```python
import math

import jax
import jax.numpy as jnp
from jax import lax
from jax.experimental import pallas as pl
from jax.experimental.pallas import tpu as pltpu
from jax.sharding import PartitionSpec as P

COLS = 1024
R_SLAB = 32
TX = 32
TY = 64
GRID_X = 16
CZ = 64
SUB = 16
NX = 4
NY = 4
NZH = 4
BLOCKS = NX * NY
SUBS = 16
HALO_Z = 8
F32 = jnp.float32
BF16 = jnp.bfloat16
MESH = pl.DeviceIdType.MESH
WIN_ROWS = (40, 32, 32, 40)
MSG_ROWS = (40, 32, 32, 40)
PAD = 64


def view_geometry(block_angles, view_id):
    angle_index = block_angles[view_id // 8] + 150 * (view_id % 8)
    angle_rad = angle_index.astype(F32) * (2.0 * math.pi / 1200.0)
    cos_part = jnp.cos(angle_rad)
    sin_part = jnp.sin(angle_rad)
    spread = jnp.maximum(jnp.abs(cos_part), jnp.abs(sin_part))
    magnify = 1.3 + 0.35 * cos_part
    return (
        cos_part,
        sin_part,
        magnify,
        magnify * spread,
        1.0 / spread,
        2.5 * sin_part,
        R_SLAB / CZ * magnify / 1.65,
    )


def snake_position(tile_id):
    grid_row = tile_id // GRID_X
    along_row = tile_id % GRID_X
    grid_col = jnp.where(grid_row % 2 == 0, along_row, GRID_X - 1 - along_row)
    return (grid_col, grid_row)


def tables(block_angles, tile_id):
    core = tile_id % 2
    chip = tile_id // 2
    zh = chip % NZH
    block = chip // NZH
    half_x = GRID_X * TX / 2
    half_y = 128 // GRID_X * TY / 2

    views = jnp.arange(128, dtype=jnp.int32)
    c, s, m, b, g, h, e = view_geometry(block_angles, views)
    chips = jnp.arange(64, dtype=jnp.int32)
    col0, row0 = snake_position(2 * chips)
    col1, _ = snake_position(2 * chips + 1)
    sx = (jnp.minimum(col0, col1) * TX).astype(F32) + 0.5 - half_x
    sy = (row0 * TY).astype(F32) + 0.5 - half_y
    corner = COLS / 2 + m[:, None] * (sx[None] * c[:, None] + sy[None] * s[:, None])
    reach = 63.0 * m * (jnp.minimum(c, 0.0) + jnp.minimum(s, 0.0)) - b / 2
    lowest = corner + reach[:, None]
    first4 = jnp.floor((lowest - 0.25) * 0.25).astype(jnp.int32)
    first4 = lax.optimization_barrier(first4)

    order = (jnp.arange(NZH, dtype=jnp.int32)[:, None] * 2 + core
             + 8 * jnp.arange(BLOCKS, dtype=jnp.int32)[None, :]).reshape(-1)
    vc, vs, vm, vb, vg, vh, ve = view_geometry(block_angles, order)
    fpar = jnp.stack(
        [vg * vm * vc, vg * vm * vs, vg, vg * jnp.minimum(vb, 1.0),
         vg * (vb + 1.0) * 0.5, vh, ve, ve],
        axis=1,
    ).reshape(-1)
    sub = jnp.arange(SUBS, dtype=jnp.int32)
    tile_of = jnp.where(sub // 8 == 0, tile_id, 2 * chip + 1 - core)
    gcol, grow = snake_position(tile_of)
    px = (gcol * TX + (sub // 4) % 2 * SUB).astype(F32) + 0.5 - half_x
    py = (grow * TY + sub % 4 * SUB).astype(F32) + 0.5 - half_y
    base = COLS / 2 + vm[:, None] * (px[None] * vc[:, None] + py[None] * vs[:, None])
    low = base + ((SUB - 1.0) * vm * (jnp.minimum(vc, 0.0) + jnp.minimum(vs, 0.0)) - vb / 2)[:, None]
    start = jnp.floor(low)
    fsub = (vg[:, None] * (base - start - 0.5)).reshape(-1)
    own_first = lax.dynamic_index_in_dim(first4, chip, 1, keepdims=False)
    own_first = own_first.reshape(BLOCKS, 8)
    own_first = lax.dynamic_slice(
        jnp.pad(own_first, ((0, 0), (0, 1))), (jnp.int32(0), core), (BLOCKS, 8))[:, ::2]
    own_first = own_first.T.reshape(-1)
    isub = (start.astype(jnp.int32) - 4 * own_first[:, None]).reshape(-1)
    mine = lax.dynamic_slice(
        jnp.pad(first4, ((0, 1), (0, 0))), (block * 8 + core, jnp.int32(0)), (8, 64))[::2]
    roff = lax.dynamic_index_in_dim(
        mine.reshape(NZH, BLOCKS, NZH), zh, 2, keepdims=False).reshape(-1)
    return fpar, fsub, isub, roff


def kernel(fpar, fsub, isub, roff, vol_ref, mask_ref, out_ref,
           own_v, pair_v, own_h, pair_h, wts, res40, res32, axial_rows,
           send0, send1, send2, send3, recv0, recv1, recv2, recv3, summed, arrived,
           vol_send, vol_recv, msg_send, msg_recv, sum_send, sum_recv):
    tile = lax.axis_index("tile")
    slab = lax.axis_index("slab")
    core = lax.rem(tile, 2)
    chip = lax.div(tile, 2)
    zh = lax.rem(chip, NZH)
    block = lax.div(chip, NZH)
    x = lax.div(block, NY)
    y = lax.rem(block, NY)
    sends = (send0, send1, send2, send3)
    recvs = (recv0, recv1, recv2, recv3)

    def device(bx, z, k):
        return (bx * NZH + z) * 2 + k

    partner = 2 * chip + 1 - core
    greeted = [(partner, slab), (tile, 1 - slab), (partner, 1 - slab)]
    for dx in range(NX):
        for dy in range(NY):
            if dx or dy:
                there = lax.rem(x + dx, NX) * NY + lax.rem(y + dy, NY)
                greeted.append((device(there, zh, core), slab))
    for dz in range(1, NZH):
        greeted.append((device(block, lax.rem(zh + dz, NZH), core), slab))
    barrier = pltpu.get_barrier_semaphore()
    for where_to in greeted:
        pl.semaphore_signal(barrier, inc=1, device_id=where_to, device_id_type=MESH)

    own_v[...] = vol_ref[...].astype(F32) * mask_ref[...].astype(F32)
    for res, win in ((res40, 40), (res32, 32)):
        pad = 2 * win

        def clear(j, carry, res=res, win=win, pad=pad):
            res[j, 0:pad, :] = jnp.zeros((pad, 128), F32)
            res[j, pad + win:, :] = jnp.zeros((pad, 128), F32)
            return carry

        lax.fori_loop(0, NY * SUBS, clear, 0)
    for zz in range(NZH):

        def clear(j, carry, zz=zz):
            recvs[zz][j, 0:PAD, :] = jnp.zeros((PAD, 128), F32)
            recvs[zz][j, PAD + MSG_ROWS[zz]:, :] = jnp.zeros((PAD, 128), F32)
            return carry

        lax.fori_loop(0, BLOCKS, clear, 0)

    pl.semaphore_wait(barrier, len(greeted))

    edge = pl.ds(pl.multiple_of((1 - slab) * (CZ - HALO_Z), HALO_Z), HALO_Z)
    give_pair = pltpu.make_async_remote_copy(
        own_v, pair_v, vol_send.at[0], vol_recv.at[0],
        device_id=(partner, slab), device_id_type=MESH)
    give_edge = pltpu.make_async_remote_copy(
        own_v.at[edge], own_h, vol_send.at[1], vol_recv.at[1],
        device_id=(tile, 1 - slab), device_id_type=MESH)
    give_cross = pltpu.make_async_remote_copy(
        own_v.at[edge], pair_h, vol_send.at[2], vol_recv.at[2],
        device_id=(partner, 1 - slab), device_id_type=MESH)
    give_edge.start()
    give_cross.start()
    give_pair.start()

    def take_tile(k, big, halo):
        for pb in range(16):
            cols = slice(pb * 128, (pb + 1) * 128)
            part = jnp.concatenate(
                [big[:, cols], halo[:, cols], jnp.zeros((128 - CZ - HALO_Z, 128), F32)], axis=0)
            turned = part.T.astype(BF16)
            for x2 in range(2):
                xb, xi = divmod(pb * 2 + x2, SUB)
                for yb in range(4):
                    rows = slice(x2 * 64 + yb * SUB, x2 * 64 + yb * SUB + SUB)
                    wts[k * 8 + xb * 4 + yb, xi * SUB:(xi + 1) * SUB, :] = turned[rows]

    give_edge.wait()
    take_tile(0, own_v, own_h)
    give_cross.wait()
    give_pair.wait()
    take_tile(1, pair_v, pair_h)

    pix = lax.broadcasted_iota(jnp.int32, (8, SUB * SUB), 1)
    pix_x = lax.div(pix, SUB).astype(F32)
    pix_y = lax.rem(pix, SUB).astype(F32)
    lane = lax.broadcasted_iota(jnp.int32, (80, 128), 1)
    zrow = lax.broadcasted_iota(jnp.int32, (80, 128), 0)
    row_low = (lax.rem(lane, R_SLAB) + slab * R_SLAB).astype(F32)
    slice_id = jnp.where(
        zrow < CZ, zrow + slab * CZ,
        jnp.where(slab == 0, zrow, zrow - HALO_Z)).astype(F32)
    z_pos = slice_id + (0.5 - CZ)

    def project(zz, dx):
        win, msg = WIN_ROWS[zz], MSG_ROWS[zz]
        res = res40 if win == 40 else res32
        pad = 2 * win
        half = 2 * msg
        krow = lax.broadcasted_iota(jnp.int32, (win, SUB * SUB), 0).astype(F32)
        bx = lax.rem(x + dx, NX)
        ids = [zz * BLOCKS + bx * NY + lax.rem(y + dy, NY) for dy in range(NY)]
        pre = []
        for v in ids:
            line = fpar[v * 8] * pix_x + fpar[v * 8 + 1] * pix_y
            pre.append(
                jnp.concatenate([line] * (win // 8), axis=0) - fpar[v * 8 + 2] * krow)
        for i in range(SUBS):
            parts = []
            for dy, v in enumerate(ids):
                dist = jnp.abs(pre[dy] + fsub[v * SUBS + i])
                parts.append(jnp.minimum(fpar[v * 8 + 4] - dist, fpar[v * 8 + 3]))
            foot = jnp.maximum(jnp.concatenate(parts, axis=0).astype(BF16), jnp.zeros((), BF16))
            got = jnp.dot(foot, wts[i], preferred_element_type=F32)
            for dy in range(NY):
                res[dy * SUBS + i, pad:pad + win, :] = got[dy * win:(dy + 1) * win]
        for dy, v in enumerate(ids):
            chunks = []
            for ch in range(2):
                total = None
                for i in range(SUBS):
                    at = pad + ch * half - isub[v * SUBS + i]
                    at = jnp.minimum(jnp.maximum(at, 0), pad + win)
                    term = res[dy * SUBS + i, pl.ds(at, half), :]
                    total = term if total is None else total + term
                chunks.append(total)
            part = jnp.concatenate(chunks, axis=0)
            high = part.astype(BF16)
            low = (part - high.astype(F32)).astype(BF16)
            h, e = fpar[v * 8 + 5], fpar[v * 8 + 6]
            centre = (R_SLAB + h) + e * z_pos
            axial = jnp.maximum(
                jnp.minimum(centre + e * 0.5, row_low + 1.0)
                - jnp.maximum(centre - e * 0.5, row_low), 0.0)
            a_high = axial.astype(BF16)
            a_low = (axial - a_high.astype(F32)).astype(BF16)
            blank = jnp.zeros((48, 128), BF16)
            a_high = jnp.concatenate([a_high, blank], axis=0)
            a_low = jnp.concatenate([a_low, blank], axis=0)
            axial_rows[dy, 0:4 * msg, :] = (
                jnp.dot(jnp.concatenate([high, low], axis=1),
                        jnp.concatenate([a_high, a_high], axis=0), preferred_element_type=F32)
                + jnp.dot(high, a_low, preferred_element_type=F32))
            quarter = lax.broadcasted_iota(jnp.int32, (msg, 128), 1)
            packed = axial_rows[dy, pl.ds(3, msg, stride=4), :]
            for q in (2, 1, 0):
                packed = jnp.where(quarter < 32 * (q + 1), axial_rows[dy, pl.ds(q, msg, stride=4), :], packed)
            sends[zz][dx * NY + dy] = packed
            away = message(zz, dx, dy)
            if dy == 0:
                @pl.when(dx == 0)
                def _():
                    keep(zz).start()

                @pl.when(dx != 0)
                def _():
                    away.start()
            else:
                away.start()

    def message(zz, dx, dy):
        there = lax.rem(x + dx, NX) * NY + lax.rem(y + dy, NY)
        return pltpu.make_async_remote_copy(
            sends[zz].at[dx * NY + dy],
            recvs[zz].at[block, pl.ds(PAD, MSG_ROWS[zz])],
            msg_send.at[zz, dx * NY + dy], msg_recv.at[zz, block],
            device_id=(device(there, zh, core), slab), device_id_type=MESH)

    def keep(zz):
        return pltpu.make_async_copy(
            sends[zz].at[0], recvs[zz].at[block, pl.ds(PAD, MSG_ROWS[zz])],
            msg_recv.at[zz, block])

    def arrival(zz, src):
        return pltpu.make_async_remote_copy(
            sends[zz].at[0], recvs[zz].at[src, pl.ds(PAD, MSG_ROWS[zz])],
            msg_send.at[zz, 0], msg_recv.at[zz, src],
            device_id=(device(src, zh, core), slab), device_id_type=MESH)

    def total_out(zz):
        return pltpu.make_async_remote_copy(
            summed.at[zz], arrived.at[zh], sum_send.at[zz], sum_recv.at[zh],
            device_id=(device(block, zz, core), slab), device_id_type=MESH)

    def total_keep(zz):
        return pltpu.make_async_copy(summed.at[zz], arrived.at[zh], sum_recv.at[zh])

    def gather_block(zz):
        msg = MSG_ROWS[zz]

        def await_one(src, carry):
            @pl.when(src == block)
            def _():
                keep(zz).wait()

            @pl.when(src != block)
            def _():
                arrival(zz, src).wait_recv()
            return carry

        lax.fori_loop(0, BLOCKS, await_one, 0)
        for ch in range(4):
            total = None
            for src in range(BLOCKS):
                at = PAD + PAD * ch - roff[zz * BLOCKS + src]
                at = jnp.minimum(jnp.maximum(at, 0), PAD + msg)
                term = recvs[zz][src, pl.ds(at, PAD), :]
                total = term if total is None else total + term
            summed[zz, ch * PAD:(ch + 1) * PAD, :] = total

        @pl.when(zh == zz)
        def _():
            total_keep(zz).start()

        @pl.when(zh != zz)
        def _():
            total_out(zz).start()

    for zz in range(NZH):
        def step(dx, carry, zz=zz):
            project(zz, dx)
            return carry

        lax.fori_loop(0, NX, step, 0)
        if zz:
            gather_block(zz - 1)
    gather_block(NZH - 1)

    def await_total(src, carry):
        @pl.when(src == zh)
        def _():
            total_keep(src).wait()

        @pl.when(src != zh)
        def _():
            pltpu.make_async_remote_copy(
                summed.at[0], arrived.at[src], sum_send.at[0], sum_recv.at[src],
                device_id=(device(block, src, core), slab), device_id_type=MESH).wait_recv()
            total_out(src).wait_send()
        return carry

    lax.fori_loop(0, NZH, await_total, 0)
    out_ref[...] = (arrived[0] + arrived[1]) + (arrived[2] + arrived[3])
    for zz in range(NZH):
        def drain(n, carry, zz=zz):
            message(zz, lax.div(n, NY), lax.rem(n, NY)).wait_send()
            return carry

        lax.fori_loop(1, BLOCKS, drain, 0)


def on_device(volume, fov_mask, block_angles, row_range):
    tile_id = lax.axis_index("tile")
    slab_id = lax.axis_index("slab")
    fpar, fsub, isub, roff = tables(block_angles, tile_id)
    smem = pl.BlockSpec(memory_space=pltpu.SMEM)
    vmem = pl.BlockSpec(memory_space=pltpu.VMEM)
    packed = pl.pallas_call(
        kernel,
        out_shape=jax.ShapeDtypeStruct((COLS // 4, 128), F32),
        in_specs=[smem] * 4 + [vmem] * 2,
        out_specs=vmem,
        scratch_shapes=[
            pltpu.VMEM((CZ, TX * TY), F32),
            pltpu.VMEM((CZ, TX * TY), F32),
            pltpu.VMEM((HALO_Z, TX * TY), F32),
            pltpu.VMEM((HALO_Z, TX * TY), F32),
            pltpu.VMEM((SUBS, SUB * SUB, 128), BF16),
            pltpu.VMEM((NY * SUBS, 200, 128), F32),
            pltpu.VMEM((NY * SUBS, 160, 128), F32),
            pltpu.VMEM((NY, 160, 128), F32),
            *[pltpu.VMEM((BLOCKS, r, 128), F32) for r in MSG_ROWS],
            *[pltpu.VMEM((BLOCKS, r + 2 * PAD, 128), F32) for r in MSG_ROWS],
            pltpu.VMEM((NZH, COLS // 4, 128), F32),
            pltpu.VMEM((NZH, COLS // 4, 128), F32),
            pltpu.SemaphoreType.DMA((3,)),
            pltpu.SemaphoreType.DMA((3,)),
            pltpu.SemaphoreType.DMA((NZH, BLOCKS)),
            pltpu.SemaphoreType.DMA((NZH, BLOCKS)),
            pltpu.SemaphoreType.DMA((NZH,)),
            pltpu.SemaphoreType.DMA((NZH,)),
        ],
        compiler_params=pltpu.CompilerParams(
            collective_id=0, has_side_effects=True, vmem_limit_bytes=52 * 1024 * 1024),
        cost_estimate=pl.CostEstimate(
            flops=64 * 16 * 40 * 256 * 128 * 2, bytes_accessed=1 << 20, transcendentals=0),
    )(fpar, fsub, isub, roff, volume[0], fov_mask)
    rows = packed.reshape(COLS // 4, 4, R_SLAB).transpose(2, 0, 1).reshape(R_SLAB, COLS)
    global_rows = slab_id * R_SLAB + jnp.arange(R_SLAB, dtype=jnp.int32)
    in_range = (global_rows >= row_range[tile_id, 0]) & (global_rows < row_range[tile_id, 1])
    return jnp.where(in_range[:, None], rows, F32(0.0))[None]


def solution(mesh):
    in_specs = (P("tile", "slab", None), P("tile", None), P(), P())
    out_specs = P("tile", "slab", None)
    return jax.shard_map(
        on_device, mesh=mesh, in_specs=in_specs, out_specs=out_specs, check_vma=False
    )
```

```python
import math

import jax
import jax.numpy as jnp
from jax import lax
from jax.experimental import pallas as pl
from jax.experimental.pallas import tpu as pltpu
from jax.sharding import PartitionSpec as P

COLS = 1024
R_SLAB = 32
TX = 32
TY = 64
GRID_X = 16
CZ = 64
SUB = 16
NX = 4
NY = 4
NZH = 4
BLOCKS = NX * NY
SUBS = 16
HALO_Z = 8
F32 = jnp.float32
BF16 = jnp.bfloat16
MESH = pl.DeviceIdType.MESH
WIN_ROWS = (40, 32, 32, 40)
MSG_ROWS = (40, 32, 32, 40)
SENT_ROWS = (37, 26, 26, 37)
PAD = 64
RECV_ROWS = tuple(r + 2 * PAD for r in MSG_ROWS)


def fill_tables(angles, tile, zh, block, core, real, whole):
    shape = (72, 128)
    row = lax.broadcasted_iota(jnp.int32, shape, 0)
    lane = lax.broadcasted_iota(jnp.int32, shape, 1)
    own = row < 64
    zz = jnp.where(own, row >> 4, row & 3)
    angle = jnp.zeros(shape, jnp.int32) + angles[block]
    for k in range(BLOCKS):
        angle = jnp.where(own & ((row & 15) == k), angles[k], angle)
    angle = angle + 150 * (2 * zz + core)
    theta = angle.astype(F32) * (2.0 * math.pi / 1200.0)
    c, s = jnp.cos(theta), jnp.sin(theta)
    spread = jnp.maximum(jnp.abs(c), jnp.abs(s))
    m = 1.3 + 0.35 * c
    b = m * spread
    g = 1.0 / spread
    sub = lane < SUBS
    chip2 = jnp.where(own, tile - core, ((lane - SUBS) * NZH + zh) * 2)
    tiles = jnp.where(sub, jnp.where(lane < 8, tile, tile + 1 - 2 * core), chip2)
    along = tiles & 15
    grow = tiles >> 4
    back = jnp.where(sub, 15, 14) - along
    gcol = jnp.where((grow & 1) == 1, back, along)
    off_x = jnp.where(sub, ((lane >> 2) & 1) * SUB, 0)
    off_y = jnp.where(sub, (lane & 3) * SUB, 0)
    px = (gcol * TX + off_x).astype(F32) + (0.5 - GRID_X * TX / 2)
    py = (grow * TY + off_y).astype(F32) + (0.5 - 128 // GRID_X * TY / 2)
    base = COLS / 2 + m * (px * c + py * s)
    extent = jnp.where(sub, SUB - 1.0, 4.0 * SUB - 1.0)
    low = base + extent * m * (jnp.minimum(c, 0.0) + jnp.minimum(s, 0.0)) - b * 0.5
    start = jnp.floor(jnp.where(sub, low, (low - 0.25) * 0.25))
    whole[...] = start.astype(jnp.int32)
    values = g * (base - start - 0.5)
    for k, value in enumerate((g * m * c, g * m * s, g, g * jnp.minimum(b, 1.0),
                               g * (b + 1.0) * 0.5, 2.5 * s, R_SLAB / CZ * m / 1.65)):
        values = jnp.where(lane == SUBS + k, value, values)
    real[...] = values


def kernel(angles, vol_ref, mask_ref, out_ref,
           real_v, whole_v, real, whole, own_v, pair_v, own_h, pair_h, wts, res40, res32, axial_rows,
           send0, send1, send2, send3, recv0, recv1, recv2, recv3, summed, arrived,
           table_sem, vol_send, vol_recv, msg_send, msg_recv, sum_send, sum_recv):
    tile = lax.axis_index("tile")
    slab = lax.axis_index("slab")
    core = lax.rem(tile, 2)
    chip = lax.div(tile, 2)
    zh = lax.rem(chip, NZH)
    block = lax.div(chip, NZH)
    x = lax.div(block, NY)
    y = lax.rem(block, NY)
    sends = (send0, send1, send2, send3)
    recvs = (recv0, recv1, recv2, recv3)

    def device(bx, z, k):
        return (bx * NZH + z) * 2 + k

    partner = 2 * chip + 1 - core
    greeted = [(partner, slab), (tile, 1 - slab), (partner, 1 - slab)]
    for dx in range(NX):
        for dy in range(NY):
            if dx or dy:
                there = lax.rem(x + dx, NX) * NY + lax.rem(y + dy, NY)
                greeted.append((device(there, zh, core), slab))
    for dz in range(1, NZH):
        greeted.append((device(block, lax.rem(zh + dz, NZH), core), slab))
    barrier = pltpu.get_barrier_semaphore()
    for where_to in greeted:
        pl.semaphore_signal(barrier, inc=1, device_id=where_to, device_id_type=MESH)

    own_v[...] = vol_ref[...].astype(F32) * mask_ref[...].astype(F32)
    pl.semaphore_wait(barrier, len(greeted))

    edge = pl.ds(pl.multiple_of((1 - slab) * (CZ - HALO_Z), HALO_Z), HALO_Z)
    give_pair = pltpu.make_async_remote_copy(
        own_v, pair_v, vol_send.at[0], vol_recv.at[0],
        device_id=(partner, slab), device_id_type=MESH)
    give_edge = pltpu.make_async_remote_copy(
        own_v.at[edge], own_h, vol_send.at[1], vol_recv.at[1],
        device_id=(tile, 1 - slab), device_id_type=MESH)
    give_cross = pltpu.make_async_remote_copy(
        own_v.at[edge], pair_h, vol_send.at[2], vol_recv.at[2],
        device_id=(partner, 1 - slab), device_id_type=MESH)
    give_edge.start()
    give_cross.start()
    give_pair.start()
    fill_tables(angles, tile, zh, block, core, real_v, whole_v)
    to_real = pltpu.make_async_copy(real_v, real, table_sem.at[0])
    to_whole = pltpu.make_async_copy(whole_v, whole, table_sem.at[1])
    to_real.start()
    to_whole.start()
    for res, win in ((res40, 40), (res32, 32)):
        pad = 2 * win

        def clear(j, carry, res=res, win=win, pad=pad):
            res[j, 0:pad, :] = jnp.zeros((pad, 128), F32)
            res[j, pad + win:, :] = jnp.zeros((pad, 128), F32)
            return carry

        lax.fori_loop(0, NY * SUBS, clear, 0)
    for zz in range(NZH):

        def clear(j, carry, zz=zz):
            recvs[zz][j, 0:PAD, :] = jnp.zeros((PAD, 128), F32)
            recvs[zz][j, PAD + SENT_ROWS[zz]:, :] = jnp.zeros((RECV_ROWS[zz] - PAD - SENT_ROWS[zz], 128), F32)
            return carry

        lax.fori_loop(0, BLOCKS, clear, 0)


    def take_tile(k, big, halo):
        for pb in range(16):
            cols = slice(pb * 128, (pb + 1) * 128)
            part = jnp.concatenate(
                [big[:, cols], halo[:, cols], jnp.zeros((128 - CZ - HALO_Z, 128), F32)], axis=0)
            turned = part.T.astype(BF16)
            for x2 in range(2):
                xb, xi = divmod(pb * 2 + x2, SUB)
                for yb in range(4):
                    rows = slice(x2 * 64 + yb * SUB, x2 * 64 + yb * SUB + SUB)
                    wts[k * 8 + xb * 4 + yb, xi * SUB:(xi + 1) * SUB, :] = turned[rows]

    to_real.wait()
    to_whole.wait()
    give_edge.wait()
    take_tile(0, own_v, own_h)
    give_cross.wait()
    give_pair.wait()
    take_tile(1, pair_v, pair_h)

    pix = lax.broadcasted_iota(jnp.int32, (8, SUB * SUB), 1)
    pix_x = lax.div(pix, SUB).astype(F32)
    pix_y = lax.rem(pix, SUB).astype(F32)
    lane = lax.broadcasted_iota(jnp.int32, (80, 128), 1)
    zrow = lax.broadcasted_iota(jnp.int32, (80, 128), 0)
    row_low = (lax.rem(lane, R_SLAB) + slab * R_SLAB).astype(F32)
    slice_id = jnp.where(
        zrow < CZ, zrow + slab * CZ,
        jnp.where(slab == 0, zrow, zrow - HALO_Z)).astype(F32)
    z_pos = slice_id + (0.5 - CZ)

    def to_block(turn, j):
        return lax.rem(x + j, NX) * NY + lax.rem(y + j + turn, NY)

    def project(zz, dx):
        win, msg = WIN_ROWS[zz], MSG_ROWS[zz]
        res = res40 if win == 40 else res32
        pad = 2 * win
        half = 2 * msg
        krow = lax.broadcasted_iota(jnp.int32, (win, SUB * SUB), 0).astype(F32)
        ids = [zz * BLOCKS + to_block(dx, dy) for dy in range(NY)]
        pre = []
        for v in ids:
            line = real[v, SUBS] * pix_x + real[v, SUBS + 1] * pix_y
            pre.append(
                jnp.concatenate([line] * (win // 8), axis=0) - real[v, SUBS + 2] * krow)
        for i in range(SUBS):
            parts = []
            for dy, v in enumerate(ids):
                dist = jnp.abs(pre[dy] + real[v, i])
                parts.append(jnp.minimum(real[v, SUBS + 4] - dist, real[v, SUBS + 3]))
            foot = jnp.maximum(jnp.concatenate(parts, axis=0).astype(BF16), jnp.zeros((), BF16))
            got = jnp.dot(foot, wts[i], preferred_element_type=F32)
            for dy in range(NY):
                res[dy * SUBS + i, pad:pad + win, :] = got[dy * win:(dy + 1) * win]
        for dy, v in enumerate(ids):
            chunks = []
            base = pad + 4 * whole[v, SUBS]
            for ch in range(2):
                total = None
                for i in range(SUBS):
                    at = base + ch * half - whole[v, i]
                    at = jnp.minimum(jnp.maximum(at, 0), pad + win)
                    term = res[dy * SUBS + i, pl.ds(at, half), :]
                    total = term if total is None else total + term
                chunks.append(total)
            part = jnp.concatenate(chunks, axis=0)
            high = part.astype(BF16)
            low = (part - high.astype(F32)).astype(BF16)
            h, e = real[v, SUBS + 5], real[v, SUBS + 6]
            centre = (R_SLAB + h) + e * z_pos
            axial = jnp.maximum(
                jnp.minimum(centre + e * 0.5, row_low + 1.0)
                - jnp.maximum(centre - e * 0.5, row_low), 0.0)
            a_high = axial.astype(BF16)
            a_low = (axial - a_high.astype(F32)).astype(BF16)
            blank = jnp.zeros((48, 128), BF16)
            a_high = jnp.concatenate([a_high, blank], axis=0)
            a_low = jnp.concatenate([a_low, blank], axis=0)
            both = jnp.concatenate([a_high, a_low], axis=1)
            rows = jnp.dot(jnp.concatenate([high, low], axis=1),
                           jnp.concatenate([both, both], axis=0), preferred_element_type=F32)
            axial_rows[dy, 0:4 * msg, :] = rows[:, :128] + rows[:, 128:]
            quarter = lax.broadcasted_iota(jnp.int32, (msg, 128), 1)
            packed = axial_rows[dy, pl.ds(3, msg, stride=4), :]
            for q in (2, 1, 0):
                packed = jnp.where(quarter < 32 * (q + 1), axial_rows[dy, pl.ds(q, msg, stride=4), :], packed)
            sends[zz][dx * NY + dy] = packed
            away = message(zz, dx, dy)
            if dy == 0:
                @pl.when(dx == 0)
                def _():
                    keep(zz).start()

                @pl.when(dx != 0)
                def _():
                    away.start()
            else:
                away.start()

    def message(zz, dx, dy):
        there = to_block(dx, dy)
        return pltpu.make_async_remote_copy(
            sends[zz].at[dx * NY + dy, pl.ds(0, SENT_ROWS[zz])],
            recvs[zz].at[block, pl.ds(PAD, SENT_ROWS[zz])],
            msg_send.at[zz, dx * NY + dy], msg_recv.at[zz, block],
            device_id=(device(there, zh, core), slab), device_id_type=MESH)

    def keep(zz):
        return pltpu.make_async_copy(
            sends[zz].at[0, pl.ds(0, SENT_ROWS[zz])], recvs[zz].at[block, pl.ds(PAD, SENT_ROWS[zz])],
            msg_recv.at[zz, block])

    def arrival(zz, src):
        return pltpu.make_async_remote_copy(
            sends[zz].at[0, pl.ds(0, SENT_ROWS[zz])], recvs[zz].at[src, pl.ds(PAD, SENT_ROWS[zz])],
            msg_send.at[zz, 0], msg_recv.at[zz, src],
            device_id=(device(src, zh, core), slab), device_id_type=MESH)

    def total_out(zz):
        return pltpu.make_async_remote_copy(
            summed.at[zz], arrived.at[zh], sum_send.at[zz], sum_recv.at[zh],
            device_id=(device(block, zz, core), slab), device_id_type=MESH)

    def total_keep(zz):
        return pltpu.make_async_copy(summed.at[zz], arrived.at[zh], sum_recv.at[zh])

    def gather_block(zz):
        msg = MSG_ROWS[zz]

        def await_one(src, carry):
            @pl.when(src == block)
            def _():
                keep(zz).wait()

            @pl.when(src != block)
            def _():
                arrival(zz, src).wait_recv()
            return carry

        lax.fori_loop(0, BLOCKS, await_one, 0)
        for ch in range(4):
            total = None
            for src in range(BLOCKS):
                at = PAD + PAD * ch - whole[64 + zz, SUBS + src]
                at = jnp.minimum(jnp.maximum(at, 0), PAD + msg)
                term = recvs[zz][src, pl.ds(at, PAD), :]
                total = term if total is None else total + term
            summed[zz, ch * PAD:(ch + 1) * PAD, :] = total

        @pl.when(zh == zz)
        def _():
            total_keep(zz).start()

        @pl.when(zh != zz)
        def _():
            total_out(zz).start()

    for zz in range(NZH):
        def step(dx, carry, zz=zz):
            project(zz, dx)
            return carry

        lax.fori_loop(0, NX, step, 0)
        if zz:
            gather_block(zz - 1)
    gather_block(NZH - 1)

    def await_total(src, carry):
        @pl.when(src == zh)
        def _():
            total_keep(src).wait()

        @pl.when(src != zh)
        def _():
            pltpu.make_async_remote_copy(
                summed.at[0], arrived.at[src], sum_send.at[0], sum_recv.at[src],
                device_id=(device(block, src, core), slab), device_id_type=MESH).wait_recv()
            total_out(src).wait_send()
        return carry

    lax.fori_loop(0, NZH, await_total, 0)
    out_ref[...] = (arrived[0] + arrived[1]) + (arrived[2] + arrived[3])
    for zz in range(NZH):
        def drain(n, carry, zz=zz):
            message(zz, lax.div(n, NY), lax.rem(n, NY)).wait_send()
            return carry

        lax.fori_loop(1, BLOCKS, drain, 0)


def on_device(volume, fov_mask, block_angles, row_range):
    tile_id = lax.axis_index("tile")
    slab_id = lax.axis_index("slab")
    smem = pl.BlockSpec(memory_space=pltpu.SMEM)
    vmem = pl.BlockSpec(memory_space=pltpu.VMEM)
    packed = pl.pallas_call(
        kernel,
        out_shape=jax.ShapeDtypeStruct((COLS // 4, 128), F32),
        in_specs=[smem] + [vmem] * 2,
        out_specs=vmem,
        scratch_shapes=[
            pltpu.VMEM((72, 128), F32),
            pltpu.VMEM((72, 128), jnp.int32),
            pltpu.SMEM((72, 128), F32),
            pltpu.SMEM((72, 128), jnp.int32),
            pltpu.VMEM((CZ, TX * TY), F32),
            pltpu.VMEM((CZ, TX * TY), F32),
            pltpu.VMEM((HALO_Z, TX * TY), F32),
            pltpu.VMEM((HALO_Z, TX * TY), F32),
            pltpu.VMEM((SUBS, SUB * SUB, 128), BF16),
            pltpu.VMEM((NY * SUBS, 200, 128), F32),
            pltpu.VMEM((NY * SUBS, 160, 128), F32),
            pltpu.VMEM((NY, 160, 128), F32),
            *[pltpu.VMEM((BLOCKS, r, 128), F32) for r in MSG_ROWS],
            *[pltpu.VMEM((BLOCKS, r, 128), F32) for r in RECV_ROWS],
            pltpu.VMEM((NZH, COLS // 4, 128), F32),
            pltpu.VMEM((NZH, COLS // 4, 128), F32),
            pltpu.SemaphoreType.DMA((2,)),
            pltpu.SemaphoreType.DMA((3,)),
            pltpu.SemaphoreType.DMA((3,)),
            pltpu.SemaphoreType.DMA((NZH, BLOCKS)),
            pltpu.SemaphoreType.DMA((NZH, BLOCKS)),
            pltpu.SemaphoreType.DMA((NZH,)),
            pltpu.SemaphoreType.DMA((NZH,)),
        ],
        compiler_params=pltpu.CompilerParams(
            collective_id=0, has_side_effects=True, vmem_limit_bytes=52 * 1024 * 1024),
        cost_estimate=pl.CostEstimate(
            flops=64 * 16 * 40 * 256 * 128 * 2, bytes_accessed=1 << 20, transcendentals=0),
    )(block_angles, volume[0], fov_mask)
    rows = packed.reshape(COLS // 4, 4, R_SLAB).transpose(2, 0, 1).reshape(R_SLAB, COLS)
    global_rows = slab_id * R_SLAB + jnp.arange(R_SLAB, dtype=jnp.int32)
    in_range = (global_rows >= row_range[tile_id, 0]) & (global_rows < row_range[tile_id, 1])
    return jnp.where(in_range[:, None], rows, F32(0.0))[None]


def solution(mesh):
    in_specs = (P("tile", "slab", None), P("tile", None), P(), P())
    out_specs = P("tile", "slab", None)
    return jax.shard_map(
        on_device, mesh=mesh, in_specs=in_specs, out_specs=out_specs, check_vma=False
    )
```

```python
import math

import jax
import jax.numpy as jnp
from jax import lax
from jax.experimental import pallas as pl
from jax.experimental.pallas import tpu as pltpu
from jax.sharding import PartitionSpec as P

COLS = 1024
R_SLAB = 32
TX = 32
TY = 64
GRID_X = 16
CZ = 64
SUB = 16
NX = 4
NY = 4
NZH = 4
BLOCKS = NX * NY
SUBS = 16
HALO_Z = 8
F32 = jnp.float32
BF16 = jnp.bfloat16
MESH = pl.DeviceIdType.MESH
WIN_ROWS = (40, 32)
MSG_ROWS = (40, 32)
SENT_ROWS = (37, 26)
LAND = 40
PAD = 64
RES_PAD = 80


def fill_tables(angles, tile, zh, block, core, real, whole):
    shape = (72, 128)
    row = lax.broadcasted_iota(jnp.int32, shape, 0)
    lane = lax.broadcasted_iota(jnp.int32, shape, 1)
    own = row < 64
    zz = jnp.where(own, row >> 4, row & 3)
    angle = jnp.zeros(shape, jnp.int32) + angles[block]
    for k in range(BLOCKS):
        angle = jnp.where(own & ((row & 15) == k), angles[k], angle)
    angle = angle + 150 * (2 * zz + core)
    theta = angle.astype(F32) * (2.0 * math.pi / 1200.0)
    c, s = jnp.cos(theta), jnp.sin(theta)
    spread = jnp.maximum(jnp.abs(c), jnp.abs(s))
    m = 1.3 + 0.35 * c
    b = m * spread
    g = 1.0 / spread
    backward = jnp.minimum(c, 0.0) + jnp.minimum(s, 0.0)

    def corner(tiles, mirror, off_x, off_y):
        along = tiles & 15
        grow = tiles >> 4
        gcol = jnp.where((grow & 1) == 1, mirror - along, along)
        px = (gcol * TX + off_x).astype(F32) + (0.5 - GRID_X * TX / 2)
        py = (grow * TY + off_y).astype(F32) + (0.5 - 128 // GRID_X * TY / 2)
        return COLS / 2 + m * (px * c + py * s)

    group = lane >> 4
    i = lane & 15
    base = corner(jnp.where(i < 8, tile, tile + 1 - 2 * core), 15,
                  ((i >> 2) & 1) * SUB, (i & 3) * SUB)
    start = jnp.floor(base + (SUB - 1.0) * m * backward - b * 0.5)
    origin = corner(jnp.where(own, tile - core, (i * NZH + zh) * 2), 14, 0, 0)
    low = origin + (4.0 * SUB - 1.0) * m * backward - b * 0.5
    first4 = jnp.floor((low - 0.25) * 0.25).astype(jnp.int32)
    msg = jnp.where((zz == 1) | (zz == 2), MSG_ROWS[1], MSG_ROWS[0])
    at = RES_PAD + 4 * first4 - start.astype(jnp.int32) + group * 2 * msg
    at = jnp.minimum(jnp.maximum(at, 0), RES_PAD + WIN_ROWS[0])
    come = jnp.minimum(jnp.maximum(PAD + PAD * (group & 3) - first4, 0), PAD + LAND)
    whole[...] = jnp.where(own, at, come)
    values = g * (base - start - 0.5)
    for k, value in enumerate((g * m * c, g * m * s, g, g * jnp.minimum(b, 1.0),
                               g * (b + 1.0) * 0.5, 2.5 * s, R_SLAB / CZ * m / 1.65)):
        values = jnp.where(lane == SUBS + k, value, values)
    real[...] = values


def kernel(angles, limits, vol_hbm, mask_hbm, out_ref,
           vol_ref, mask_ref, real_v, whole_v, real, whole, own_v, pair_v, own_h, pair_h,
           wts, res_a, res_b, axial_rows, sends, lands, spread, summed, arrived,
           in_sem, table_sem, vol_send, vol_recv, msg_send, msg_recv, sum_send, sum_recv):
    tile = lax.axis_index("tile")
    slab = lax.axis_index("slab")
    core = lax.rem(tile, 2)
    chip = lax.div(tile, 2)
    zh = lax.rem(chip, NZH)
    block = lax.div(chip, NZH)
    x = lax.div(block, NY)
    y = lax.rem(block, NY)
    get_vol = pltpu.make_async_copy(vol_hbm.at[0], vol_ref, in_sem.at[0])
    get_mask = pltpu.make_async_copy(mask_hbm, mask_ref, in_sem.at[1])
    get_vol.start()
    get_mask.start()

    def flipped(turn):
        mask = lax.rem(turn + 1, 4)
        high = lax.rem(lax.div(zh, 2) + lax.div(mask, 2), 2)
        low = lax.rem(lax.rem(zh, 2) + lax.rem(mask, 2), 2)
        return 2 * high + low

    def device(bx, z, k):
        return (bx * NZH + z) * 2 + k

    partner = 2 * chip + 1 - core
    greeted = [(partner, slab), (tile, 1 - slab), (partner, 1 - slab)]
    for dx in range(NX):
        for dy in range(NY):
            if dx or dy:
                there = lax.rem(x + dx, NX) * NY + lax.rem(y + dy, NY)
                greeted.append((device(there, zh, core), slab))
    for turn in range(NZH - 1):
        greeted.append((device(block, flipped(turn), core), slab))
    barrier = pltpu.get_barrier_semaphore()
    for where_to in greeted:
        pl.semaphore_signal(barrier, inc=1, device_id=where_to, device_id_type=MESH)

    get_vol.wait()
    get_mask.wait()
    own_v[...] = vol_ref[...].astype(F32) * mask_ref[...].astype(F32)
    pl.semaphore_wait(barrier, len(greeted))

    edge = pl.ds(pl.multiple_of((1 - slab) * (CZ - HALO_Z), HALO_Z), HALO_Z)
    give_pair = pltpu.make_async_remote_copy(
        own_v, pair_v, vol_send.at[0], vol_recv.at[0],
        device_id=(partner, slab), device_id_type=MESH)
    give_edge = pltpu.make_async_remote_copy(
        own_v.at[edge], own_h, vol_send.at[1], vol_recv.at[1],
        device_id=(tile, 1 - slab), device_id_type=MESH)
    give_cross = pltpu.make_async_remote_copy(
        own_v.at[edge], pair_h, vol_send.at[2], vol_recv.at[2],
        device_id=(partner, 1 - slab), device_id_type=MESH)
    give_edge.start()
    give_cross.start()
    give_pair.start()
    fill_tables(angles, tile, zh, block, core, real_v, whole_v)
    to_real = pltpu.make_async_copy(real_v, real, table_sem.at[0])
    to_whole = pltpu.make_async_copy(whole_v, whole, table_sem.at[1])
    to_real.start()
    to_whole.start()
    for res in (res_a, res_b):

        def clear(j, carry, res=res):
            res[j, 0:RES_PAD, :] = jnp.zeros((RES_PAD, 128), F32)
            res[j, RES_PAD + 32:, :] = jnp.zeros((RES_PAD + 8, 128), F32)
            return carry

        lax.fori_loop(0, 2 * SUBS, clear, 0)
    def clear(j, carry):
        spread[j, 0:PAD, :] = jnp.zeros((PAD, 128), F32)
        spread[j, PAD + LAND:, :] = jnp.zeros((PAD, 128), F32)
        for zz in range(NZH):
            sent = SENT_ROWS[int(zz in (1, 2))]
            lands[zz, j, sent:LAND, :] = jnp.zeros((LAND - sent, 128), F32)
        return carry

    lax.fori_loop(0, BLOCKS, clear, 0)
    def take_tile(k, big, halo):
        for pb in range(16):
            cols = slice(pb * 128, (pb + 1) * 128)
            part = jnp.concatenate(
                [big[:, cols], halo[:, cols], jnp.zeros((128 - CZ - HALO_Z, 128), F32)], axis=0)
            turned = part.T.astype(BF16)
            for x2 in range(2):
                xb, xi = divmod(pb * 2 + x2, SUB)
                for yb in range(4):
                    rows = slice(x2 * 64 + yb * SUB, x2 * 64 + yb * SUB + SUB)
                    wts[k * 8 + xb * 4 + yb, xi * SUB:(xi + 1) * SUB, :] = turned[rows]

    to_real.wait()
    to_whole.wait()
    give_edge.wait()
    take_tile(0, own_v, own_h)
    give_cross.wait()
    give_pair.wait()
    take_tile(1, pair_v, pair_h)

    pix = lax.broadcasted_iota(jnp.int32, (8, SUB * SUB), 1)
    pix_x = lax.div(pix, SUB).astype(F32)
    pix_y = lax.rem(pix, SUB).astype(F32)
    lane = lax.broadcasted_iota(jnp.int32, (80, 128), 1)
    zrow = lax.broadcasted_iota(jnp.int32, (80, 128), 0)
    row_low = (lax.rem(lane, R_SLAB) + slab * R_SLAB).astype(F32)
    slice_id = jnp.where(
        zrow < CZ, zrow + slab * CZ,
        jnp.where(slab == 0, zrow, zrow - HALO_Z)).astype(F32)
    z_pos = slice_id + (0.5 - CZ)

    def to_block(turn, j):
        return lax.rem(x + j, NX) * NY + lax.rem(y + j + turn, NY)

    def views(zz, turn, half):
        return [zz * BLOCKS + to_block(turn, j) for j in (2 * half, 2 * half + 1)]

    def footprints(kind, zz, turn, half, res):
        win = WIN_ROWS[kind]
        ids = views(zz, turn, half)
        krow = lax.broadcasted_iota(jnp.int32, (win, SUB * SUB), 0).astype(F32)
        pre, caps = [], []
        for v in ids:
            line = real[v, SUBS] * pix_x + real[v, SUBS + 1] * pix_y
            pre.append(
                jnp.concatenate([line] * (win // 8), axis=0) - real[v, SUBS + 2] * krow)
            caps.append(jnp.full((win, SUB * SUB), real[v, SUBS + 3], F32))
        cap = jnp.concatenate(caps, axis=0).astype(BF16)
        for i in range(SUBS):
            parts = []
            for k, v in enumerate(ids):
                parts.append(real[v, SUBS + 4] - jnp.abs(pre[k] + real[v, i]))
            foot = jnp.concatenate(parts, axis=0).astype(BF16)
            foot = jnp.maximum(jnp.minimum(foot, cap), jnp.zeros((), BF16))
            got = jnp.dot(foot, wts[i], preferred_element_type=F32)
            for k in range(2):
                res[k * SUBS + i, RES_PAD:RES_PAD + win, :] = got[k * win:(k + 1) * win]
                if win < WIN_ROWS[0]:
                    res[k * SUBS + i, RES_PAD + win:RES_PAD + WIN_ROWS[0], :] = jnp.zeros(
                        (WIN_ROWS[0] - win, 128), F32)
            yield

    def messages(kind, zz, turn, half, res):
        msg = MSG_ROWS[kind]
        reach = 2 * msg
        for k, v in enumerate(views(zz, turn, half)):
            chunks = []
            for ch in range(2):
                total = None
                for i in range(SUBS):
                    term = res[k * SUBS + i, pl.ds(whole[v, ch * SUBS + i], reach), :]
                    total = term if total is None else total + term
                    if i % 5 == 4:
                        yield
                chunks.append(total)
            part = jnp.concatenate(chunks, axis=0)
            high = part.astype(BF16)
            low = (part - high.astype(F32)).astype(BF16)
            h, e = real[v, SUBS + 5], real[v, SUBS + 6]
            centre = (R_SLAB + h) + e * z_pos
            axial = jnp.maximum(
                jnp.minimum(centre + e * 0.5, row_low + 1.0)
                - jnp.maximum(centre - e * 0.5, row_low), 0.0)
            a_high = axial.astype(BF16)
            a_low = (axial - a_high.astype(F32)).astype(BF16)
            blank = jnp.zeros((48, 128), BF16)
            a_high = jnp.concatenate([a_high, blank], axis=0)
            a_low = jnp.concatenate([a_low, blank], axis=0)
            both = jnp.concatenate([a_high, a_low], axis=1)
            rows = jnp.dot(jnp.concatenate([high, low], axis=1),
                           jnp.concatenate([both, both], axis=0), preferred_element_type=F32)
            at = 2 * half + k
            axial_rows[at, 0:4 * msg, :] = rows[:, :128] + rows[:, 128:]
            yield
            quarter = lax.broadcasted_iota(jnp.int32, (msg, 128), 1)
            packed = axial_rows[at, pl.ds(3, msg, stride=4), :]
            for q in (2, 1, 0):
                packed = jnp.where(
                    quarter < 32 * (q + 1), axial_rows[at, pl.ds(q, msg, stride=4), :], packed)
            sends[zz, turn * NY + at, 0:msg, :] = packed
            yield

    def together(*works):
        works = list(works)
        while works:
            for work in list(works):
                if next(work, works) is works:
                    works.remove(work)

    def message(kind, zz, turn, j):
        rows = SENT_ROWS[kind]
        return pltpu.make_async_remote_copy(
            sends.at[zz, turn * NY + j, pl.ds(0, rows)], lands.at[zz, block, pl.ds(0, rows)],
            msg_send.at[zz, turn * NY + j], msg_recv.at[zz, block],
            device_id=(device(to_block(turn, j), zh, core), slab), device_id_type=MESH)

    def keep(kind, zz):
        rows = SENT_ROWS[kind]
        return pltpu.make_async_copy(
            sends.at[zz, 0, pl.ds(0, rows)], lands.at[zz, block, pl.ds(0, rows)],
            msg_recv.at[zz, block])

    def arrival(kind, zz, src):
        rows = SENT_ROWS[kind]
        return pltpu.make_async_remote_copy(
            sends.at[zz, 0, pl.ds(0, rows)], lands.at[zz, src, pl.ds(0, rows)],
            msg_send.at[zz, 0], msg_recv.at[zz, src],
            device_id=(device(src, zh, core), slab), device_id_type=MESH)

    def total_out(turn):
        return pltpu.make_async_remote_copy(
            summed.at[turn], arrived.at[turn], sum_send.at[turn], sum_recv.at[turn],
            device_id=(device(block, flipped(turn), core), slab), device_id_type=MESH)

    def octant(kind, zz):
        def step(turn, carry):
            before = jnp.maximum(turn - 1, 0)
            together(footprints(kind, zz, turn, 0, res_a), messages(kind, zz, before, 1, res_b))

            @pl.when(turn > 0)
            def _():
                message(kind, zz, turn - 1, 2).start()
                message(kind, zz, turn - 1, 3).start()

            together(footprints(kind, zz, turn, 1, res_b), messages(kind, zz, turn, 0, res_a))

            @pl.when(turn == 0)
            def _():
                keep(kind, zz).start()

            @pl.when(turn > 0)
            def _():
                message(kind, zz, turn, 0).start()

            message(kind, zz, turn, 1).start()
            return carry

        lax.fori_loop(0, NX, step, 0)
        together(messages(kind, zz, NX - 1, 1, res_b))
        message(kind, zz, NX - 1, 2).start()
        message(kind, zz, NX - 1, 3).start()

    def by_kind(zz, work):
        narrow = (zz == 1) | (zz == 2)

        @pl.when(narrow)
        def _():
            work(1)

        @pl.when(jnp.logical_not(narrow))
        def _():
            work(0)

    def gather_block(turn):
        zz = flipped(turn)

        def await_all(kind):
            def await_one(src, carry):
                @pl.when(src == block)
                def _():
                    keep(kind, zz).wait()

                @pl.when(src != block)
                def _():
                    arrival(kind, zz, src).wait_recv()
                return carry

            lax.fori_loop(0, BLOCKS, await_one, 0)

        by_kind(zz, await_all)
        for src in range(BLOCKS):
            spread[src, PAD:PAD + LAND, :] = lands[zz, src]
        for ch in range(4):
            total = None
            for src in range(BLOCKS):
                term = spread[src, pl.ds(whole[64 + zz, 64 + ch * BLOCKS + src], PAD), :]
                total = term if total is None else total + term
            summed[turn, ch * PAD:(ch + 1) * PAD, :] = total

    def one_octant(turn, carry):
        zz = flipped(turn)
        by_kind(zz, lambda kind: octant(kind, zz))

        @pl.when(turn > 0)
        def _():
            gather_block(turn - 1)
            total_out(turn - 1).start()
        return carry

    lax.fori_loop(0, NZH, one_octant, 0)
    gather_block(NZH - 1)
    for turn in range(NZH - 1):
        total_out(turn).wait()
    out_row = lax.rem(lax.broadcasted_iota(jnp.int32, (COLS // 4, 128), 1), R_SLAB) + slab * R_SLAB
    read_out = (out_row >= limits[tile, 0]) & (out_row < limits[tile, 1])
    total = (arrived[0] + arrived[1]) + (arrived[2] + summed[NZH - 1])
    out_ref[...] = jnp.where(read_out, total, 0.0)
    for zz in range(NZH):
        def drain(n, carry, zz=zz):
            message(int(zz in (1, 2)), zz, lax.div(n, NY), lax.rem(n, NY)).wait_send()
            return carry

        lax.fori_loop(1, BLOCKS, drain, 0)


def on_device(volume, fov_mask, block_angles, row_range):
    smem = pl.BlockSpec(memory_space=pltpu.SMEM)
    anywhere = pl.BlockSpec(memory_space=pl.ANY)
    pixels = TX * TY
    packed = pl.pallas_call(
        kernel,
        out_shape=jax.ShapeDtypeStruct((COLS // 4, 128), F32),
        in_specs=[smem, smem, anywhere, anywhere],
        out_specs=pl.BlockSpec(memory_space=pltpu.VMEM),
        scratch_shapes=[
            pltpu.VMEM((CZ, pixels), BF16),
            pltpu.VMEM((1, pixels), jnp.int32),
            pltpu.VMEM((72, 128), F32),
            pltpu.VMEM((72, 128), jnp.int32),
            pltpu.SMEM((72, 128), F32),
            pltpu.SMEM((72, 128), jnp.int32),
            pltpu.VMEM((CZ, pixels), F32),
            pltpu.VMEM((CZ, pixels), F32),
            pltpu.VMEM((HALO_Z, pixels), F32),
            pltpu.VMEM((HALO_Z, pixels), F32),
            pltpu.VMEM((SUBS, SUB * SUB, 128), BF16),
            pltpu.VMEM((2 * SUBS, 2 * RES_PAD + 40, 128), F32),
            pltpu.VMEM((2 * SUBS, 2 * RES_PAD + 40, 128), F32),
            pltpu.VMEM((NY, 160, 128), F32),
            pltpu.VMEM((NZH, BLOCKS, LAND, 128), F32),
            pltpu.VMEM((NZH, BLOCKS, LAND, 128), F32),
            pltpu.VMEM((BLOCKS, LAND + 2 * PAD, 128), F32),
            pltpu.VMEM((NZH, COLS // 4, 128), F32),
            pltpu.VMEM((NZH - 1, COLS // 4, 128), F32),
            pltpu.SemaphoreType.DMA((2,)),
            pltpu.SemaphoreType.DMA((2,)),
            pltpu.SemaphoreType.DMA((3,)),
            pltpu.SemaphoreType.DMA((3,)),
            pltpu.SemaphoreType.DMA((NZH, BLOCKS)),
            pltpu.SemaphoreType.DMA((NZH, BLOCKS)),
            pltpu.SemaphoreType.DMA((NZH - 1,)),
            pltpu.SemaphoreType.DMA((NZH - 1,)),
        ],
        compiler_params=pltpu.CompilerParams(
            collective_id=0, has_side_effects=True, vmem_limit_bytes=44 * 1024 * 1024),
        cost_estimate=pl.CostEstimate(
            flops=64 * 16 * 40 * 256 * 128 * 2, bytes_accessed=1 << 20, transcendentals=0),
    )(block_angles, row_range, volume, fov_mask)
    return packed.reshape(COLS // 4, 4, R_SLAB).transpose(2, 0, 1).reshape(1, R_SLAB, COLS)


def solution(mesh):
    in_specs = (P("tile", "slab", None), P("tile", None), P(), P())
    out_specs = P("tile", "slab", None)
    return jax.shard_map(
        on_device, mesh=mesh, in_specs=in_specs, out_specs=out_specs, check_vma=False
    )
```

```python
import math

import jax
import jax.numpy as jnp
import numpy as np
from jax import lax
from jax.experimental import pallas as pl
from jax.experimental.pallas import tpu as pltpu
from jax.sharding import PartitionSpec as P

COLS = 1024
R_SLAB = 32
TX = 32
TY = 64
GRID_X = 16
CZ = 64
SUB = 16
NX = 4
NY = 4
NZH = 4
BLOCKS = NX * NY
SUBS = 16
HALO_Z = 8
F32 = jnp.float32
BF16 = jnp.bfloat16
MESH = pl.DeviceIdType.MESH
WIN_ROWS = (40, 32)
MSG_ROWS = (40, 32)
SENT_ROWS = (37, 26)
LAND = 40
SPANS = ((0, 256), (24, 232))
PAD = 64
RES_PAD = 120
RES_ROWS = RES_PAD + 160


def window_rows(kind):
    octants = ((0, 1, 6, 7), (2, 3, 4, 5))[kind]
    index = np.concatenate([np.arange(151) + 150 * o for o in octants])
    c, s = np.cos(index * (2 * np.pi / 1200)), np.sin(index * (2 * np.pi / 1200))
    m = 1.3 + 0.35 * c
    primary = m * np.maximum(np.abs(c), np.abs(s))
    second = m * np.minimum(np.abs(c), np.abs(s))
    need = (15 * (primary + second) + primary).max() + 2.0
    spans = []
    for a in range(4):
        for d in range(4):
            shift = SUB * (a * primary + d * second)
            low = max(int((shift.min() - 1.0) // 8) * 8, 0)
            top = shift.max() + 4.5
            high = min(-int(-(top + need) // 8) * 8, 4 * MSG_ROWS[kind])
            assert top - low < RES_PAD and high - shift.min() + 1 < RES_PAD + 40
            assert 0 <= low and high <= 160
            spans.append((low, high))
    return spans


def fill_tables(angles, tile, zh, block, core, real, whole):
    shape = (72, 128)
    row = lax.broadcasted_iota(jnp.int32, shape, 0)
    lane = lax.broadcasted_iota(jnp.int32, shape, 1)
    own = row < 64
    zz = jnp.where(own, row >> 4, row & 3)
    angle = jnp.zeros(shape, jnp.int32) + angles[block]
    for k in range(BLOCKS):
        angle = jnp.where(own & ((row & 15) == k), angles[k], angle)
    angle = angle + 150 * (2 * zz + core)
    theta = angle.astype(F32) * (2.0 * math.pi / 1200.0)
    c, s = jnp.cos(theta), jnp.sin(theta)
    spread = jnp.maximum(jnp.abs(c), jnp.abs(s))
    m = 1.3 + 0.35 * c
    b = m * spread
    g = 1.0 / spread
    backward = jnp.minimum(c, 0.0) + jnp.minimum(s, 0.0)

    def corner(tiles, off_x, off_y):
        along = tiles & 15
        grow = tiles >> 4
        gcol = jnp.where((grow & 1) == 1, 14 - along, along)
        px = (gcol * TX + off_x).astype(F32) + (0.5 - GRID_X * TX / 2)
        py = (grow * TY + off_y).astype(F32) + (0.5 - 128 // GRID_X * TY / 2)
        return COLS / 2 + m * (px * c + py * s)

    group = lane >> 4
    i = lane & 15
    along_x = ((zz + core) & 1) == 0
    narrow = (zz == 1) | (zz == 2)
    step_x = jnp.where(along_x, i >> 2, i & 3)
    step_y = jnp.where(along_x, i & 3, i >> 2)
    step_x = jnp.where(narrow, 3 - step_x, step_x)
    step_y = jnp.where(zz >= 2, 3 - step_y, step_y)
    base = corner(tile - core + 0 * lane, step_x * SUB, step_y * SUB)
    start = jnp.floor(base + (SUB - 1.0) * m * backward - b * 0.5)
    origin = corner(jnp.where(own, tile - core, (i * NZH + zh) * 2), 0, 0)
    low = origin + (4.0 * SUB - 1.0) * m * backward - b * 0.5
    first4 = jnp.floor((low - 0.25) * 0.25).astype(jnp.int32)
    at = RES_PAD + 4 * first4 - start.astype(jnp.int32)
    at = jnp.minimum(jnp.maximum(at, 0), RES_PAD)
    come = jnp.minimum(jnp.maximum(PAD + PAD * (group & 3) - first4, 0), PAD + LAND)
    whole[...] = jnp.where(own, at, come)
    values = g * (base - start - 0.5)
    for k, value in enumerate((g * m * c, g * m * s, g, g * jnp.minimum(b, 1.0),
                               g * (b + 1.0) * 0.5, 2.5 * s, R_SLAB / CZ * m / 1.65)):
        values = jnp.where(lane == SUBS + k, value, values)
    real[...] = values


def kernel(angles, limits, vol_hbm, mask_hbm, out_ref,
           vol_ref, mask_ref, real_v, whole_v, real, whole, own_v, pair_v, own_h, pair_h,
           wts, res_a, res_b, axial_rows, sends, lands, spread, summed, arrived,
           in_sem, table_sem, vol_send, vol_recv, msg_send, msg_recv, sum_send, sum_recv):
    tile = lax.axis_index("tile")
    slab = lax.axis_index("slab")
    core = lax.rem(tile, 2)
    chip = lax.div(tile, 2)
    zh = lax.rem(chip, NZH)
    block = lax.div(chip, NZH)
    x = lax.div(block, NY)
    y = lax.rem(block, NY)
    get_vol = pltpu.make_async_copy(vol_hbm.at[0], vol_ref, in_sem.at[0])
    get_mask = pltpu.make_async_copy(mask_hbm, mask_ref, in_sem.at[1])
    get_vol.start()
    get_mask.start()

    def flipped(turn):
        mask = lax.rem(lax.rem(turn + 1, 4) * 2 + lax.div(lax.rem(turn + 1, 4), 2), 4)
        high = lax.rem(lax.div(zh, 2) + lax.div(mask, 2), 2)
        low = lax.rem(lax.rem(zh, 2) + lax.rem(mask, 2), 2)
        return 2 * high + low

    def device(bx, z, k):
        return (bx * NZH + z) * 2 + k

    partner = 2 * chip + 1 - core
    greeted = [(partner, slab), (tile, 1 - slab), (partner, 1 - slab)]
    for dx in range(NX):
        for dy in range(NY):
            if dx or dy:
                there = lax.rem(x + dx, NX) * NY + lax.rem(y + dy, NY)
                greeted.append((device(there, zh, core), slab))
    for turn in range(NZH - 1):
        greeted.append((device(block, flipped(turn), core), slab))
    barrier = pltpu.get_barrier_semaphore()
    for where_to in greeted:
        pl.semaphore_signal(barrier, inc=1, device_id=where_to, device_id_type=MESH)

    get_vol.wait()
    get_mask.wait()
    own_v[...] = vol_ref[...].astype(F32) * mask_ref[...].astype(F32)
    pl.semaphore_wait(barrier, len(greeted))

    edge = pl.ds(pl.multiple_of((1 - slab) * (CZ - HALO_Z), HALO_Z), HALO_Z)
    give_pair = pltpu.make_async_remote_copy(
        own_v, pair_v, vol_send.at[0], vol_recv.at[0],
        device_id=(partner, slab), device_id_type=MESH)
    give_edge = pltpu.make_async_remote_copy(
        own_v.at[edge], own_h, vol_send.at[1], vol_recv.at[1],
        device_id=(tile, 1 - slab), device_id_type=MESH)
    give_cross = pltpu.make_async_remote_copy(
        own_v.at[edge], pair_h, vol_send.at[2], vol_recv.at[2],
        device_id=(partner, 1 - slab), device_id_type=MESH)
    give_edge.start()
    give_cross.start()
    give_pair.start()
    fill_tables(angles, tile, zh, block, core, real_v, whole_v)
    to_real = pltpu.make_async_copy(real_v, real, table_sem.at[0])
    to_whole = pltpu.make_async_copy(whole_v, whole, table_sem.at[1])
    to_real.start()
    to_whole.start()
    for res in (res_a, res_b):

        def clear(j, carry, res=res):
            res[j, 0:RES_PAD, :] = jnp.zeros((RES_PAD, 128), F32)
            res[j, RES_PAD + 32:, :] = jnp.zeros((RES_ROWS - RES_PAD - 32, 128), F32)
            return carry

        lax.fori_loop(0, 2 * SUBS, clear, 0)
    def clear(j, carry):
        spread[j, 0:PAD, :] = jnp.zeros((PAD, 128), F32)
        spread[j, PAD + LAND:, :] = jnp.zeros((PAD, 128), F32)
        for zz in range(NZH):
            sent = SENT_ROWS[int(zz in (1, 2))]
            lands[zz, j, sent:LAND, :] = jnp.zeros((LAND - sent, 128), F32)
        return carry

    lax.fori_loop(0, BLOCKS, clear, 0)
    def take_tile(side, big, halo):
        for pb in range(16):
            cols = slice(pb * 128, (pb + 1) * 128)
            part = jnp.concatenate(
                [big[:, cols], halo[:, cols], jnp.zeros((128 - CZ - HALO_Z, 128), F32)], axis=0)
            turned = part.T.astype(BF16)
            for x2 in range(2):
                xb, xi = divmod(pb * 2 + x2, SUB)
                for yb in range(4):
                    rows = slice(x2 * 64 + yb * SUB, x2 * 64 + yb * SUB + SUB)
                    wts[(2 * side + xb) * 4 + yb, xi * SUB:(xi + 1) * SUB, :] = turned[rows]

    to_real.wait()
    to_whole.wait()
    give_edge.wait()
    side = lax.rem(core + lax.div(tile, GRID_X), 2)
    take_tile(side, own_v, own_h)
    give_cross.wait()
    give_pair.wait()
    take_tile(1 - side, pair_v, pair_h)

    pix = lax.broadcasted_iota(jnp.int32, (8, SUB * SUB), 1)
    pix_x = lax.div(pix, SUB).astype(F32)
    pix_y = lax.rem(pix, SUB).astype(F32)
    zlane = lax.broadcasted_iota(jnp.int32, (R_SLAB, 128), 1)
    row_low = (lax.broadcasted_iota(jnp.int32, (R_SLAB, 128), 0) + slab * R_SLAB).astype(F32)
    slice_id = jnp.where(
        zlane < CZ, zlane + slab * CZ,
        jnp.where(slab == 0, zlane, zlane - HALO_Z)).astype(F32)
    z_pos = slice_id + (0.5 - CZ)

    def to_block(turn, j):
        return lax.rem(x + j, NX) * NY + lax.rem(y + j + turn, NY)

    def weight_of(zz, i):
        a, d = divmod(i, 4)
        along_x = 1 - lax.rem(zz + core, 2)
        narrow = lax.rem(zz, 2) + lax.div(zz, 2) - 2 * lax.rem(zz, 2) * lax.div(zz, 2)
        late = lax.div(zz, 2)
        step_x = along_x * a + (1 - along_x) * d
        step_y = along_x * d + (1 - along_x) * a
        step_x = narrow * (3 - 2 * step_x) + step_x
        step_y = late * (3 - 2 * step_y) + step_y
        return 4 * step_x + step_y

    def views(zz, turn, half):
        return [zz * BLOCKS + to_block(turn, j) for j in (2 * half, 2 * half + 1)]

    def footprints(kind, zz, turn, half, res):
        win = WIN_ROWS[kind]
        ids = views(zz, turn, half)
        krow = lax.broadcasted_iota(jnp.int32, (win, SUB * SUB), 0).astype(F32)
        pre, caps = [], []
        for v in ids:
            line = real[v, SUBS] * pix_x + real[v, SUBS + 1] * pix_y
            pre.append(
                jnp.concatenate([line] * (win // 8), axis=0) - real[v, SUBS + 2] * krow)
            caps.append(jnp.full((win, SUB * SUB), real[v, SUBS + 3], F32))
        cap = jnp.concatenate(caps, axis=0).astype(BF16)
        for i in range(SUBS):
            parts = []
            for k, v in enumerate(ids):
                parts.append(real[v, SUBS + 4] - jnp.abs(pre[k] + real[v, i]))
            foot = jnp.concatenate(parts, axis=0).astype(BF16)
            foot = jnp.maximum(jnp.minimum(foot, cap), jnp.zeros((), BF16))
            got = jnp.dot(foot, wts[weight_of(zz, i)], preferred_element_type=F32)
            for k in range(2):
                res[k * SUBS + i, RES_PAD:RES_PAD + win, :] = got[k * win:(k + 1) * win]
                if win < WIN_ROWS[0]:
                    res[k * SUBS + i, RES_PAD + win:RES_PAD + WIN_ROWS[0], :] = jnp.zeros(
                        (WIN_ROWS[0] - win, 128), F32)
            yield

    def messages(kind, zz, turn, half, res):
        msg = MSG_ROWS[kind]
        spans = window_rows(kind)
        for k, v in enumerate(views(zz, turn, half)):
            groups = [None] * (msg // 2)
            for i, (first, end) in enumerate(spans):
                term = res[k * SUBS + i, pl.ds(whole[v, i] + first, end - first), :]
                for n in range(first // 8, end // 8):
                    piece = term[8 * n - first:8 * n - first + 8]
                    groups[n] = piece if groups[n] is None else groups[n] + piece
                if i % 3 == 2:
                    yield
            blank = jnp.zeros((8, 128), F32)
            part = jnp.concatenate([blank if g is None else g for g in groups], axis=0)
            high = part.astype(BF16)
            low = (part - high.astype(F32)).astype(BF16)
            h, e = real[v, SUBS + 5], real[v, SUBS + 6]
            centre = (R_SLAB + h) + e * z_pos
            axial = jnp.maximum(
                jnp.minimum(centre + e * 0.5, row_low + 1.0)
                - jnp.maximum(centre - e * 0.5, row_low), 0.0)
            a_high = axial.astype(BF16)
            a_low = (axial - a_high.astype(F32)).astype(BF16)
            a_high = jnp.concatenate([jnp.concatenate([a_high] * 4, axis=0)] * 2, axis=1)
            a_low = jnp.concatenate([jnp.concatenate([a_low] * 4, axis=0)] * 2, axis=1)
            rows = lax.dot_general(
                jnp.concatenate([high, low], axis=1), jnp.concatenate([a_high, a_low], axis=0),
                (((1,), (1,)), ((), ())), preferred_element_type=F32)
            at = 2 * half + k
            axial_rows[at, 0:4 * msg, :] = rows[:, :128] + rows[:, 128:]
            yield
            quarter = lax.broadcasted_iota(jnp.int32, (msg, 128), 1)
            packed = axial_rows[at, pl.ds(3, msg, stride=4), :]
            for q in (2, 1, 0):
                packed = jnp.where(
                    quarter < 32 * (q + 1), axial_rows[at, pl.ds(q, msg, stride=4), :], packed)
            sends[zz, turn * NY + at, 0:msg, :] = packed
            yield

    def together(*works):
        works = list(works)
        while works:
            for work in list(works):
                if next(work, works) is works:
                    works.remove(work)

    def message(kind, zz, turn, j):
        rows = SENT_ROWS[kind]
        return pltpu.make_async_remote_copy(
            sends.at[zz, turn * NY + j, pl.ds(0, rows)], lands.at[zz, block, pl.ds(0, rows)],
            msg_send.at[zz], msg_recv.at[zz],
            device_id=(device(to_block(turn, j), zh, core), slab), device_id_type=MESH)

    def keep(kind, zz):
        rows = SENT_ROWS[kind]
        return pltpu.make_async_copy(
            sends.at[zz, 0, pl.ds(0, rows)], lands.at[zz, block, pl.ds(0, rows)],
            msg_recv.at[zz])

    def all_arrived(kind, zz):
        rows = pl.ds(0, SENT_ROWS[kind])
        return pltpu.make_async_copy(sends.at[zz, :, rows], lands.at[zz, :, rows], msg_recv.at[zz])

    def all_sent(kind, zz):
        rows, others = pl.ds(0, SENT_ROWS[kind]), pl.ds(1, BLOCKS - 1)
        return pltpu.make_async_copy(
            lands.at[zz, others, rows], sends.at[zz, others, rows], msg_send.at[zz])

    def total_out(kind, turn):
        rows = pl.ds(SPANS[kind][0], SPANS[kind][1] - SPANS[kind][0])
        return pltpu.make_async_remote_copy(
            summed.at[turn, rows], arrived.at[turn, rows], sum_send.at[turn], sum_recv.at[turn],
            device_id=(device(block, flipped(turn), core), slab), device_id_type=MESH)

    def half_octant(kind, zz, late):
        def step(turn, carry):
            before = jnp.maximum(turn - 1, 0)
            together(footprints(kind, zz, turn, 0, res_a), messages(kind, zz, before, 1, res_b))
            together(footprints(kind, zz, turn, 1, res_b), messages(kind, zz, turn, 0, res_a))
            message(kind, zz, turn, 1).start()

            @pl.when(turn == 0)
            def _():
                keep(kind, zz).start()

            @pl.when(turn > 0)
            def _():
                message(kind, zz, turn, 0).start()
                message(kind, zz, turn - 1, 2).start()
                message(kind, zz, turn - 1, 3).start()
            return carry

        lax.fori_loop(2 * late, 2 * late + 2, step, 0)

        @pl.when(late == 1)
        def _():
            together(messages(kind, zz, NX - 1, 1, res_b))
            message(kind, zz, NX - 1, 2).start()
            message(kind, zz, NX - 1, 3).start()

    def by_kind(zz, work):
        narrow = (zz == 1) | (zz == 2)

        @pl.when(narrow)
        def _():
            work(1)

        @pl.when(jnp.logical_not(narrow))
        def _():
            work(0)

    def gather_block(turn):
        zz = flipped(turn)

        by_kind(zz, lambda kind: all_arrived(kind, zz).wait())
        for src in range(BLOCKS):
            spread[src, PAD:PAD + LAND, :] = lands[zz, src]
        for ch in range(4):
            total = None
            for src in range(BLOCKS):
                term = spread[src, pl.ds(whole[64 + zz, 64 + ch * BLOCKS + src], PAD), :]
                total = term if total is None else total + term
            summed[turn, ch * PAD:(ch + 1) * PAD, :] = total

    def advance(n, carry):
        turn, late = lax.div(n, 2), lax.rem(n, 2)
        zz = flipped(turn)
        by_kind(zz, lambda kind: half_octant(kind, zz, late))

        @pl.when((n == 3) | (n == 5) | (n == 6))
        def _():
            gather_block(turn - 1)
            by_kind(flipped(turn - 1), lambda kind: total_out(kind, turn - 1).start())
        return carry

    lax.fori_loop(0, 2 * NZH, advance, 0)
    gather_block(NZH - 1)
    for turn in range(NZH - 1):
        by_kind(flipped(turn), lambda kind, turn=turn: total_out(kind, turn).wait_send())
    out_row = lax.rem(lax.broadcasted_iota(jnp.int32, (COLS // 4, 128), 1), R_SLAB) + slab * R_SLAB
    read_out = (out_row >= limits[0, tile]) & (out_row < limits[1, tile])

    def finish(kind):
        first, end = SPANS[kind]
        for turn in range(NZH - 1):
            total_out(kind, turn).wait_recv()
        total = (arrived[0, first:end] + arrived[1, first:end]) + (
            arrived[2, first:end] + summed[NZH - 1, first:end])
        if first:
            edge = jnp.zeros((first, 128), F32)
            total = jnp.concatenate([edge, total, edge], axis=0)
        out_ref[...] = jnp.where(read_out, total, 0.0)

    by_kind(zh, finish)
    for zz in range(NZH):
        all_sent(int(zz in (1, 2)), zz).wait()


def on_device(volume, fov_mask, block_angles, row_range):
    smem = pl.BlockSpec(memory_space=pltpu.SMEM)
    anywhere = pl.BlockSpec(memory_space=pltpu.HBM)
    pixels = TX * TY
    packed = pl.pallas_call(
        kernel,
        out_shape=jax.ShapeDtypeStruct((COLS // 4, 128), F32),
        in_specs=[smem, smem, anywhere, anywhere],
        out_specs=pl.BlockSpec(memory_space=pltpu.VMEM),
        scratch_shapes=[
            pltpu.VMEM((CZ, pixels), BF16),
            pltpu.VMEM((1, pixels), jnp.int32),
            pltpu.VMEM((72, 128), F32),
            pltpu.VMEM((72, 128), jnp.int32),
            pltpu.SMEM((72, 128), F32),
            pltpu.SMEM((72, 128), jnp.int32),
            pltpu.VMEM((CZ, pixels), F32),
            pltpu.VMEM((CZ, pixels), F32),
            pltpu.VMEM((HALO_Z, pixels), F32),
            pltpu.VMEM((HALO_Z, pixels), F32),
            pltpu.VMEM((SUBS, SUB * SUB, 128), BF16),
            pltpu.VMEM((2 * SUBS, RES_ROWS, 128), F32),
            pltpu.VMEM((2 * SUBS, RES_ROWS, 128), F32),
            pltpu.VMEM((NY, 160, 128), F32),
            pltpu.VMEM((NZH, BLOCKS, LAND, 128), F32),
            pltpu.VMEM((NZH, BLOCKS, LAND, 128), F32),
            pltpu.VMEM((BLOCKS, LAND + 2 * PAD, 128), F32),
            pltpu.VMEM((NZH, COLS // 4, 128), F32),
            pltpu.VMEM((NZH - 1, COLS // 4, 128), F32),
            pltpu.SemaphoreType.DMA((2,)),
            pltpu.SemaphoreType.DMA((2,)),
            pltpu.SemaphoreType.DMA((3,)),
            pltpu.SemaphoreType.DMA((3,)),
            pltpu.SemaphoreType.DMA((NZH,)),
            pltpu.SemaphoreType.DMA((NZH,)),
            pltpu.SemaphoreType.DMA((NZH - 1,)),
            pltpu.SemaphoreType.DMA((NZH - 1,)),
        ],
        compiler_params=pltpu.CompilerParams(
            collective_id=0, has_side_effects=True, vmem_limit_bytes=54912 * 1024),
        cost_estimate=pl.CostEstimate(
            flops=64 * 16 * 40 * 256 * 128 * 2, bytes_accessed=1 << 20, transcendentals=0),
    )(block_angles, row_range.T, volume, fov_mask)
    return packed.reshape(COLS // 4, 4, R_SLAB).transpose(2, 0, 1).reshape(1, R_SLAB, COLS)


def solution(mesh):
    in_specs = (P("tile", "slab", None), P("tile", None), P(), P())
    out_specs = P("tile", "slab", None)
    return jax.shard_map(
        on_device, mesh=mesh, in_specs=in_specs, out_specs=out_specs, check_vma=False
    )
```

```python
import math

import jax
import jax.numpy as jnp
import numpy as np
from jax import lax
from jax.experimental import pallas as pl
from jax.experimental.pallas import tpu as pltpu
from jax.sharding import PartitionSpec as P

COLS = 1024
R_SLAB = 32
TX = 32
TY = 64
GRID_X = 16
CZ = 64
SUB = 16
NX = 4
NY = 4
NZH = 4
BLOCKS = NX * NY
SUBS = 16
HALO_Z = 8
F32 = jnp.float32
BF16 = jnp.bfloat16
MESH = pl.DeviceIdType.MESH
WIN_ROWS = (40, 32)
MSG_ROWS = (40, 32)
SENT_ROWS = (37, 26)
LAND = 40
SPANS = ((0, 256), (24, 232))
PAD = 64
RES_PAD = 120
RES_ROWS = RES_PAD + 160


def window_rows(kind):
    octants = ((0, 1, 6, 7), (2, 3, 4, 5))[kind]
    index = np.concatenate([np.arange(151) + 150 * o for o in octants])
    c, s = np.cos(index * (2 * np.pi / 1200)), np.sin(index * (2 * np.pi / 1200))
    m = 1.3 + 0.35 * c
    primary = m * np.maximum(np.abs(c), np.abs(s))
    second = m * np.minimum(np.abs(c), np.abs(s))
    need = (15 * (primary + second) + primary).max() + 2.0
    spans = []
    for a in range(4):
        for d in range(4):
            shift = SUB * (a * primary + d * second)
            low = max(int((shift.min() - 1.0) // 8) * 8, 0)
            top = shift.max() + 4.5
            high = min(-int(-(top + need) // 8) * 8, 4 * MSG_ROWS[kind])
            assert top - low < RES_PAD and high - shift.min() + 1 < RES_PAD + 40
            assert 0 <= low and high <= 160
            spans.append((low, high))
    return spans


def fill_tables(angles, tile, zh, block, core, real, whole):
    shape = (72, 128)
    row = lax.broadcasted_iota(jnp.int32, shape, 0)
    lane = lax.broadcasted_iota(jnp.int32, shape, 1)
    own = row < 64
    zz = jnp.where(own, row >> 4, row & 3)
    angle = jnp.zeros(shape, jnp.int32) + angles[block]
    for k in range(BLOCKS):
        angle = jnp.where(own & ((row & 15) == k), angles[k], angle)
    angle = angle + 150 * (2 * zz + core)
    theta = angle.astype(F32) * (2.0 * math.pi / 1200.0)
    c, s = jnp.cos(theta), jnp.sin(theta)
    spread = jnp.maximum(jnp.abs(c), jnp.abs(s))
    m = 1.3 + 0.35 * c
    b = m * spread
    g = 1.0 / spread
    backward = jnp.minimum(c, 0.0) + jnp.minimum(s, 0.0)

    def corner(tiles, off_x, off_y):
        along = tiles & 15
        grow = tiles >> 4
        gcol = jnp.where((grow & 1) == 1, 14 - along, along)
        px = (gcol * TX + off_x).astype(F32) + (0.5 - GRID_X * TX / 2)
        py = (grow * TY + off_y).astype(F32) + (0.5 - 128 // GRID_X * TY / 2)
        return COLS / 2 + m * (px * c + py * s)

    group = lane >> 4
    i = lane & 15
    along_x = ((zz + core) & 1) == 0
    narrow = (zz == 1) | (zz == 2)
    step_x = jnp.where(along_x, i >> 2, i & 3)
    step_y = jnp.where(along_x, i & 3, i >> 2)
    step_x = jnp.where(narrow, 3 - step_x, step_x)
    step_y = jnp.where(zz >= 2, 3 - step_y, step_y)
    base = corner(tile - core + 0 * lane, step_x * SUB, step_y * SUB)
    start = jnp.floor(base + (SUB - 1.0) * m * backward - b * 0.5)
    origin = corner(jnp.where(own, tile - core, (i * NZH + zh) * 2), 0, 0)
    low = origin + (4.0 * SUB - 1.0) * m * backward - b * 0.5
    first4 = jnp.floor((low - 0.25) * 0.25).astype(jnp.int32)
    at = RES_PAD + 4 * first4 - start.astype(jnp.int32)
    at = jnp.minimum(jnp.maximum(at, 0), RES_PAD)
    come = jnp.minimum(jnp.maximum(PAD + PAD * (group & 3) - first4, 0), PAD + LAND)
    whole[...] = jnp.where(own, at, come)
    values = g * (base - start - 0.5)
    for k, value in enumerate((g * m * c, g * m * s, g, g * jnp.minimum(b, 1.0),
                               g * (b + 1.0) * 0.5, 2.5 * s, R_SLAB / CZ * m / 1.65)):
        values = jnp.where(lane == SUBS + k, value, values)
    real[...] = values


def kernel(angles, limits, vol_hbm, mask_hbm, out_ref,
           vol_ref, mask_ref, real_v, whole_v, real, whole, own_v, pair_v, own_h, pair_h,
           wts, res_a, res_b, axial_rows, sends, lands, spread, summed, arrived,
           in_sem, table_sem, vol_send, vol_recv, msg_send, msg_recv, sum_send, sum_recv):
    tile = lax.axis_index("tile")
    slab = lax.axis_index("slab")
    core = lax.rem(tile, 2)
    chip = lax.div(tile, 2)
    zh = lax.rem(chip, NZH)
    block = lax.div(chip, NZH)
    x = lax.div(block, NY)
    y = lax.rem(block, NY)
    get_vol = pltpu.make_async_copy(vol_hbm.at[0], vol_ref, in_sem.at[0])
    get_mask = pltpu.make_async_copy(mask_hbm, mask_ref, in_sem.at[1])
    get_vol.start()
    get_mask.start()

    def flipped(turn):
        mask = lax.rem(lax.rem(turn + 1, 4) * 2 + lax.div(lax.rem(turn + 1, 4), 2), 4)
        high = lax.rem(lax.div(zh, 2) + lax.div(mask, 2), 2)
        low = lax.rem(lax.rem(zh, 2) + lax.rem(mask, 2), 2)
        return 2 * high + low

    def device(bx, z, k):
        return (bx * NZH + z) * 2 + k

    partner = 2 * chip + 1 - core
    greeted = [(partner, slab), (tile, 1 - slab), (partner, 1 - slab)]
    for dx in range(NX):
        for dy in range(NY):
            if dx or dy:
                there = lax.rem(x + dx, NX) * NY + lax.rem(y + dy, NY)
                greeted.append((device(there, zh, core), slab))
    for turn in range(NZH - 1):
        greeted.append((device(block, flipped(turn), core), slab))
    barrier = pltpu.get_barrier_semaphore()
    for where_to in greeted:
        pl.semaphore_signal(barrier, inc=1, device_id=where_to, device_id_type=MESH)

    get_vol.wait()
    get_mask.wait()
    own_v[...] = vol_ref[...].astype(F32) * mask_ref[...].astype(F32)
    pl.semaphore_wait(barrier, len(greeted))

    edge = pl.ds(pl.multiple_of((1 - slab) * (CZ - HALO_Z), HALO_Z), HALO_Z)
    give_pair = pltpu.make_async_remote_copy(
        own_v, pair_v, vol_send.at[0], vol_recv.at[0],
        device_id=(partner, slab), device_id_type=MESH)
    give_edge = pltpu.make_async_remote_copy(
        own_v.at[edge], own_h, vol_send.at[1], vol_recv.at[1],
        device_id=(tile, 1 - slab), device_id_type=MESH)
    give_cross = pltpu.make_async_remote_copy(
        own_v.at[edge], pair_h, vol_send.at[2], vol_recv.at[2],
        device_id=(partner, 1 - slab), device_id_type=MESH)
    give_edge.start()
    give_cross.start()
    give_pair.start()
    fill_tables(angles, tile, zh, block, core, real_v, whole_v)
    to_real = pltpu.make_async_copy(real_v, real, table_sem.at[0])
    to_whole = pltpu.make_async_copy(whole_v, whole, table_sem.at[1])
    to_real.start()
    to_whole.start()
    for res in (res_a, res_b):

        def clear(j, carry, res=res):
            res[j, 0:RES_PAD, :] = jnp.zeros((RES_PAD, 128), F32)
            res[j, RES_PAD + 32:, :] = jnp.zeros((RES_ROWS - RES_PAD - 32, 128), F32)
            return carry

        lax.fori_loop(0, 2 * SUBS, clear, 0)
    def clear(j, carry):
        spread[j, 0:PAD, :] = jnp.zeros((PAD, 128), F32)
        spread[j, PAD + LAND:, :] = jnp.zeros((PAD, 128), F32)
        for zz in range(NZH):
            sent = SENT_ROWS[int(zz in (1, 2))]
            lands[zz, j, sent:LAND, :] = jnp.zeros((LAND - sent, 128), F32)
        return carry

    lax.fori_loop(0, BLOCKS, clear, 0)
    def take_tile(side, big, halo):
        for pb in range(16):
            cols = slice(pb * 128, (pb + 1) * 128)
            part = jnp.concatenate(
                [big[:, cols], halo[:, cols], jnp.zeros((128 - CZ - HALO_Z, 128), F32)], axis=0)
            turned = part.T.astype(BF16)
            for x2 in range(2):
                xb, xi = divmod(pb * 2 + x2, SUB)
                for yb in range(4):
                    rows = slice(x2 * 64 + yb * SUB, x2 * 64 + yb * SUB + SUB)
                    wts[(2 * side + xb) * 4 + yb, xi * SUB:(xi + 1) * SUB, :] = turned[rows]

    to_real.wait()
    to_whole.wait()
    give_edge.wait()
    side = lax.rem(core + lax.div(tile, GRID_X), 2)
    take_tile(side, own_v, own_h)
    give_cross.wait()
    give_pair.wait()
    take_tile(1 - side, pair_v, pair_h)

    pix = lax.broadcasted_iota(jnp.int32, (8, SUB * SUB), 1)
    pix_x = lax.div(pix, SUB).astype(F32)
    pix_y = lax.rem(pix, SUB).astype(F32)
    zlane = lax.broadcasted_iota(jnp.int32, (R_SLAB, 128), 1)
    row_low = (lax.broadcasted_iota(jnp.int32, (R_SLAB, 128), 0) + slab * R_SLAB).astype(F32)
    slice_id = jnp.where(
        zlane < CZ, zlane + slab * CZ,
        jnp.where(slab == 0, zlane, zlane - HALO_Z)).astype(F32)
    z_pos = slice_id + (0.5 - CZ)

    def to_block(turn, j):
        return lax.rem(x + j, NX) * NY + lax.rem(y + j + turn, NY)

    def weight_of(zz, i):
        a, d = divmod(i, 4)
        along_x = 1 - lax.rem(zz + core, 2)
        narrow = lax.rem(zz, 2) + lax.div(zz, 2) - 2 * lax.rem(zz, 2) * lax.div(zz, 2)
        late = lax.div(zz, 2)
        step_x = along_x * a + (1 - along_x) * d
        step_y = along_x * d + (1 - along_x) * a
        step_x = narrow * (3 - 2 * step_x) + step_x
        step_y = late * (3 - 2 * step_y) + step_y
        return 4 * step_x + step_y

    def views(zz, turn, half):
        return [zz * BLOCKS + to_block(turn, j) for j in (2 * half, 2 * half + 1)]

    def footprints(kind, zz, turn, half, res):
        win = WIN_ROWS[kind]
        ids = views(zz, turn, half)
        krow = lax.broadcasted_iota(jnp.int32, (win, SUB * SUB), 0).astype(F32)
        pre, caps = [], []
        for v in ids:
            line = real[v, SUBS] * pix_x + real[v, SUBS + 1] * pix_y
            pre.append(
                jnp.concatenate([line] * (win // 8), axis=0) - real[v, SUBS + 2] * krow)
            caps.append(jnp.full((win, SUB * SUB), real[v, SUBS + 3], F32))
        cap = jnp.concatenate(caps, axis=0).astype(BF16)
        for i in range(SUBS):
            parts = []
            for k, v in enumerate(ids):
                parts.append(real[v, SUBS + 4] - jnp.abs(pre[k] + real[v, i]))
            foot = jnp.concatenate(parts, axis=0).astype(BF16)
            foot = jnp.maximum(jnp.minimum(foot, cap), jnp.zeros((), BF16))
            got = jnp.dot(foot, wts[weight_of(zz, i)], preferred_element_type=F32)
            for k in range(2):
                res[k * SUBS + i, RES_PAD:RES_PAD + win, :] = got[k * win:(k + 1) * win]
                if win < WIN_ROWS[0]:
                    res[k * SUBS + i, RES_PAD + win:RES_PAD + WIN_ROWS[0], :] = jnp.zeros(
                        (WIN_ROWS[0] - win, 128), F32)
            yield

    def messages(kind, zz, turn, half, res):
        msg = MSG_ROWS[kind]
        spans = window_rows(kind)
        for k, v in enumerate(views(zz, turn, half)):
            groups = [None] * (msg // 2)
            for i, (first, end) in enumerate(spans):
                term = res[k * SUBS + i, pl.ds(whole[v, i] + first, end - first), :]
                for n in range(first // 8, end // 8):
                    piece = term[8 * n - first:8 * n - first + 8]
                    groups[n] = piece if groups[n] is None else groups[n] + piece
                if i % 3 == 2:
                    yield
            blank = jnp.zeros((8, 128), F32)
            part = jnp.concatenate([blank if g is None else g for g in groups], axis=0)
            high = part.astype(BF16)
            low = (part - high.astype(F32)).astype(BF16)
            h, e = real[v, SUBS + 5], real[v, SUBS + 6]
            centre = (R_SLAB + h) + e * z_pos
            axial = jnp.maximum(
                jnp.minimum(centre + e * 0.5, row_low + 1.0)
                - jnp.maximum(centre - e * 0.5, row_low), 0.0)
            a_high = axial.astype(BF16)
            a_low = (axial - a_high.astype(F32)).astype(BF16)
            a_high = jnp.concatenate([jnp.concatenate([a_high] * 4, axis=0)] * 2, axis=1)
            a_low = jnp.concatenate([jnp.concatenate([a_low] * 4, axis=0)] * 2, axis=1)
            rows = lax.dot_general(
                jnp.concatenate([high, low], axis=1), jnp.concatenate([a_high, a_low], axis=0),
                (((1,), (1,)), ((), ())), preferred_element_type=F32)
            at = 2 * half + k
            axial_rows[at, 0:4 * msg, :] = rows[:, :128] + rows[:, 128:]
            yield
            quarter = lax.broadcasted_iota(jnp.int32, (msg, 128), 1)
            packed = axial_rows[at, pl.ds(3, msg, stride=4), :]
            for q in (2, 1, 0):
                packed = jnp.where(
                    quarter < 32 * (q + 1), axial_rows[at, pl.ds(q, msg, stride=4), :], packed)
            sends[zz, turn * NY + at, 0:msg, :] = packed
            yield

    def together(*works):
        works = list(works)
        while works:
            for work in list(works):
                if next(work, works) is works:
                    works.remove(work)

    def message(kind, zz, turn, j):
        rows = SENT_ROWS[kind]
        return pltpu.make_async_remote_copy(
            sends.at[zz, turn * NY + j, pl.ds(0, rows)], lands.at[zz, block, pl.ds(0, rows)],
            msg_send.at[zz], msg_recv.at[zz],
            device_id=(device(to_block(turn, j), zh, core), slab), device_id_type=MESH)

    def keep(kind, zz):
        rows = SENT_ROWS[kind]
        return pltpu.make_async_copy(
            sends.at[zz, 0, pl.ds(0, rows)], lands.at[zz, block, pl.ds(0, rows)],
            msg_recv.at[zz])

    def all_arrived(kind, zz):
        rows = pl.ds(0, SENT_ROWS[kind])
        return pltpu.make_async_copy(sends.at[zz, :, rows], lands.at[zz, :, rows], msg_recv.at[zz])

    def all_sent(kind, zz):
        rows, others = pl.ds(0, SENT_ROWS[kind]), pl.ds(1, BLOCKS - 1)
        return pltpu.make_async_copy(
            lands.at[zz, others, rows], sends.at[zz, others, rows], msg_send.at[zz])

    def total_out(kind, turn):
        rows = pl.ds(SPANS[kind][0], SPANS[kind][1] - SPANS[kind][0])
        return pltpu.make_async_remote_copy(
            summed.at[turn, rows], arrived.at[turn, rows], sum_send.at[turn], sum_recv.at[turn],
            device_id=(device(block, flipped(turn), core), slab), device_id_type=MESH)

    def half_octant(kind, zz, late):
        def step(turn, carry):
            before = jnp.maximum(turn - 1, 0)
            together(footprints(kind, zz, turn, 0, res_a), messages(kind, zz, before, 1, res_b))
            together(footprints(kind, zz, turn, 1, res_b), messages(kind, zz, turn, 0, res_a))
            message(kind, zz, turn, 1).start()

            @pl.when(turn == 0)
            def _():
                keep(kind, zz).start()

            @pl.when(turn > 0)
            def _():
                message(kind, zz, turn, 0).start()
                message(kind, zz, turn - 1, 2).start()
                message(kind, zz, turn - 1, 3).start()
            return carry

        lax.fori_loop(2 * late, 2 * late + 2, step, 0)

        @pl.when(late == 1)
        def _():
            together(messages(kind, zz, NX - 1, 1, res_b))
            message(kind, zz, NX - 1, 2).start()
            message(kind, zz, NX - 1, 3).start()

    def by_kind(zz, work):
        narrow = (zz == 1) | (zz == 2)

        @pl.when(narrow)
        def _():
            work(1)

        @pl.when(jnp.logical_not(narrow))
        def _():
            work(0)

    def gather_block(turn):
        zz = flipped(turn)

        by_kind(zz, lambda kind: all_arrived(kind, zz).wait())
        for src in range(BLOCKS):
            spread[src, PAD:PAD + LAND, :] = lands[zz, src]
        for ch in range(4):
            total = None
            for src in range(BLOCKS):
                term = spread[src, pl.ds(whole[64 + zz, 64 + ch * BLOCKS + src], PAD), :]
                total = term if total is None else total + term
            summed[turn, ch * PAD:(ch + 1) * PAD, :] = total

    def advance(n, carry):
        turn, late = lax.div(n, 2), lax.rem(n, 2)
        zz = flipped(turn)
        by_kind(zz, lambda kind: half_octant(kind, zz, late))

        @pl.when((n == 3) | (n == 5) | (n == 6))
        def _():
            gather_block(turn - 1)
            by_kind(flipped(turn - 1), lambda kind: total_out(kind, turn - 1).start())
        return carry

    lax.fori_loop(0, 2 * NZH, advance, 0)
    gather_block(NZH - 1)
    for turn in range(NZH - 1):
        by_kind(flipped(turn), lambda kind, turn=turn: total_out(kind, turn).wait_send())
    out_row = lax.rem(lax.broadcasted_iota(jnp.int32, (COLS // 4, 128), 1), R_SLAB) + slab * R_SLAB
    read_out = (out_row >= limits[0, tile]) & (out_row < limits[1, tile])

    def finish(kind):
        first, end = SPANS[kind]
        for turn in range(NZH - 1):
            total_out(kind, turn).wait_recv()
        total = (arrived[0, first:end] + arrived[1, first:end]) + (
            arrived[2, first:end] + summed[NZH - 1, first:end])
        if first:
            edge = jnp.zeros((first, 128), F32)
            total = jnp.concatenate([edge, total, edge], axis=0)
        out_ref[...] = jnp.where(read_out, total, 0.0)

    by_kind(zh, finish)
    for zz in range(NZH):
        all_sent(int(zz in (1, 2)), zz).wait()


def on_device(volume, fov_mask, block_angles, row_range):
    smem = pl.BlockSpec(memory_space=pltpu.SMEM)
    anywhere = pl.BlockSpec(memory_space=pltpu.HBM)
    pixels = TX * TY
    packed = pl.pallas_call(
        kernel,
        out_shape=jax.ShapeDtypeStruct((COLS // 4, 128), F32),
        in_specs=[smem, smem, anywhere, anywhere],
        out_specs=pl.BlockSpec(memory_space=pltpu.VMEM),
        scratch_shapes=[
            pltpu.VMEM((CZ, pixels), BF16),
            pltpu.VMEM((1, pixels), jnp.int32),
            pltpu.VMEM((72, 128), F32),
            pltpu.VMEM((72, 128), jnp.int32),
            pltpu.SMEM((72, 128), F32),
            pltpu.SMEM((72, 128), jnp.int32),
            pltpu.VMEM((CZ, pixels), F32),
            pltpu.VMEM((CZ, pixels), F32),
            pltpu.VMEM((HALO_Z, pixels), F32),
            pltpu.VMEM((HALO_Z, pixels), F32),
            pltpu.VMEM((SUBS, SUB * SUB, 128), BF16),
            pltpu.VMEM((2 * SUBS, RES_ROWS, 128), F32),
            pltpu.VMEM((2 * SUBS, RES_ROWS, 128), F32),
            pltpu.VMEM((NY, 168, 128), F32),
            pltpu.VMEM((NZH, BLOCKS, LAND, 128), F32),
            pltpu.VMEM((NZH, BLOCKS, LAND, 128), F32),
            pltpu.VMEM((BLOCKS, LAND + 2 * PAD, 128), F32),
            pltpu.VMEM((NZH, COLS // 4, 128), F32),
            pltpu.VMEM((NZH - 1, COLS // 4, 128), F32),
            pltpu.SemaphoreType.DMA((2,)),
            pltpu.SemaphoreType.DMA((2,)),
            pltpu.SemaphoreType.DMA((3,)),
            pltpu.SemaphoreType.DMA((3,)),
            pltpu.SemaphoreType.DMA((NZH,)),
            pltpu.SemaphoreType.DMA((NZH,)),
            pltpu.SemaphoreType.DMA((NZH - 1,)),
            pltpu.SemaphoreType.DMA((NZH - 1,)),
        ],
        compiler_params=pltpu.CompilerParams(
            collective_id=0, has_side_effects=True, vmem_limit_bytes=54912 * 1024),
        cost_estimate=pl.CostEstimate(
            flops=64 * 16 * 40 * 256 * 128 * 2, bytes_accessed=1 << 20, transcendentals=0),
    )(block_angles, row_range.T, volume, fov_mask)
    return packed.reshape(COLS // 4, 4, R_SLAB).transpose(2, 0, 1).reshape(1, R_SLAB, COLS)


def solution(mesh):
    in_specs = (P("tile", "slab", None), P("tile", None), P(), P())
    out_specs = P("tile", "slab", None)
    return jax.shard_map(
        on_device, mesh=mesh, in_specs=in_specs, out_specs=out_specs, check_vma=False
    )
```
